128 devices in a mesh: group: 16 (over y_hi, x, core), inner: 8 (over y_lo, z).
Axes of the slice: x: 4, y: 4 (y_hi: 2, y_lo: 2; y = y_hi * 2 + y_lo), z: 4, core: 2. Of those that a mesh axis runs over, the one named last changes fastest.
Arguments:
- latents: bfloat16 [128, 1536, 640], P(('group', 'inner')), may hold values from -45 to 45
- cotangent: bfloat16 [128, 1536, 640], P(('group', 'inner')), may hold values from -6 to 6
- gain: float32 [640], replicated, may hold values from 0.25 to 1.75
- bias: float32 [640], replicated, may hold values from -3 to 3
- weight: float32 [16, 5760, 640], P('group', 'inner'), may hold values from -6 to 6
- momentum: float32 [16, 5760, 640], P('group', 'inner'), may hold values from -6 to 6
- step: int32 [1], replicated, may hold values from 0 to 999
Outputs:
- block_out: bfloat16 [128, 1536, 640], P(('group', 'inner'))
- new_weight: float32 [16, 5760, 640], P('group', 'inner')
- new_momentum: float32 [16, 5760, 640], P('group', 'inner')
The draws below stay inside these ranges and needn't reach their ends.
All inputs are finite; a program needn't handle non-finite values.
Results may differ from the reference program's by a relative error of at most 0.014.
Values may be sent and summed in bfloat16 or wider, within the bound.
No kernel may reach another device: no remote copies, remote signals or barrier semaphores. Data moves between devices by JAX's collectives and lax.ppermute only.
A program may use at most 256 MiB of HBM per device.

```python
import math
import jax
import jax.numpy as jnp
from jax import lax

C = 640
GN_GROUPS = 32
HEIGHT = 48
WIDTH = 32
KROWS = 5760
IMAGES = 128
N_GROUP = 16


def draw_latents(key, part):
    key = jax.random.fold_in(key, 5)
    shape = (IMAGES, HEIGHT * WIDTH, C)
    first = jax.random.fold_in(key, 1)
    second = jax.random.fold_in(key, 2)
    third = jax.random.fold_in(key, 3)
    fourth = jax.random.fold_in(key, 4)
    base = jnp.clip(jax.random.normal(first, shape, jnp.float32), -4.0, 4.0)
    pixel_scale = jnp.exp(jax.random.uniform(second, (IMAGES, HEIGHT * WIDTH, 1), jnp.float32, 0.0, math.log(3.16)))
    offset = jax.random.uniform(fourth, (IMAGES, 1, C), jnp.float32, -1.0, 1.0)
    chan_scale = jnp.exp(jax.random.uniform(third, (1, 1, C), jnp.float32, 0.0, math.log(3.16)))
    return (base * pixel_scale * chan_scale + offset).astype(jnp.bfloat16)


def block_levels(rng, dims, shards, low, largest):
    loudness, own = 1.0, jax.random.fold_in(rng, 6)
    for position, blocks in shards:
        steps = jnp.exp(jax.random.uniform(jax.random.fold_in(own, position), (blocks,), jnp.float32, low / len(shards), largest / len(shards)))
        loudness = loudness * jnp.repeat(steps, dims[position] // blocks).reshape([-1 if axis == position else 1 for axis in range(len(dims))])
    return loudness


def bell_draw(own_key, shape, scale, limit, shards=(), kind=jnp.bfloat16):
    entries = jax.random.normal(own_key, shape, jnp.float32) * scale
    if len(shards) > 0:
        entries = block_levels(own_key, shape, shards, -0.22, 0.18) * entries
    return jnp.clip(entries, min=-limit, max=limit).astype(kind)


def setup_inputs(seed: int = 0) -> dict:
    seeds = jax.random.split(jax.random.key(seed), 8)
    return {
        "latents": draw_latents(jax.random.fold_in(seeds[7], 71), 0),
        "cotangent": bell_draw(seeds[1], (IMAGES, HEIGHT * WIDTH, C), 1.0, 6.0, ((0, 128),)),
        "gain": jnp.clip(1.0 + 0.15 * jax.random.normal(seeds[2], (C,), jnp.float32), 0.25, 1.75),
        "bias": bell_draw(seeds[3], (C,), 0.5, 3.0, (), jnp.float32),
        "weight": bell_draw(seeds[4], (N_GROUP, KROWS, C), 1.0, 6.0, ((0, 16), (1, 8)), jnp.float32),
        "momentum": bell_draw(seeds[5], (N_GROUP, KROWS, C), 1.0, 6.0, ((0, 16), (1, 8)), jnp.float32),
        "step": jax.random.randint(seeds[6], (1,), 0, 1000).astype(jnp.int32),
    }


def norm_act(latents, gain, bias):
    count, pixels, chans = latents.shape
    values = latents.astype(jnp.float32).reshape(count, pixels, GN_GROUPS, chans // GN_GROUPS)
    center = lax.optimization_barrier(jnp.mean(values, axis=(1, 3), keepdims=True))
    spread = lax.optimization_barrier(jnp.mean((values - center) * (values - center), axis=(1, 3), keepdims=True))
    normed = ((values - center) * lax.rsqrt(spread + 1e-05)).reshape(count, pixels, chans) * gain + bias
    return jax.nn.silu(normed).astype(jnp.bfloat16)

def unfold(hidden):
    count, pixels, chans = hidden.shape
    image = hidden.reshape(count, HEIGHT, WIDTH, chans)
    padded = jnp.pad(image, ((0, 0), (1, 1), (1, 1), (0, 0)))
    taps = [padded[:, a:a + HEIGHT, b:b + WIDTH, :] for a in range(3) for b in range(3)]
    return jnp.concatenate(taps, axis=-1).reshape(count * pixels, 9 * chans)

def reference(latents, cotangent, gain, bias, weight, momentum, step):
    groups = weight.shape[0]
    inner_count = latents.shape[0] // groups
    chans = latents.shape[2]
    scale = (9 * chans) ** (-0.5)
    grouped = latents.reshape(groups, inner_count, latents.shape[1], chans)
    grouped_cot = cotangent.reshape(groups, inner_count, latents.shape[1], chans)

    def one_group(items):
        lat_g, cot_g, weight_g = items
        columns = unfold(norm_act(lat_g, gain, bias))
        conv = scale * jnp.dot(columns, weight_g.astype(jnp.bfloat16), preferred_element_type=jnp.float32)
        block = (lat_g.astype(jnp.float32) + conv.reshape(lat_g.shape)).astype(jnp.bfloat16)
        upstream = cot_g.reshape(-1, chans)
        grad = scale * lax.dot_general(columns, upstream, (((0,), (0,)), ((), ())), preferred_element_type=jnp.float32)
        return (block, grad)
    blocks, grads = lax.map(one_group, (grouped, grouped_cot, weight))
    moved = 0.9 * momentum + grads
    stepped = weight - 0.05 * moved
    levels = groups.bit_length() - 1
    distance = jnp.left_shift(jnp.int32(1), (step[0] % levels).astype(jnp.int32))
    partner = (jnp.arange(groups, dtype=jnp.int32) + distance) % groups
    new_weight = 0.5 * (stepped + stepped[partner])
    new_momentum = 0.5 * (moved + moved[partner])
    return (blocks.reshape(latents.shape), new_weight, new_momentum)
```

```python
from functools import partial

import jax
import jax.numpy as jnp
from jax import lax
from jax.experimental import pallas as pl
from jax.experimental.pallas import tpu as pltpu
from jax.sharding import PartitionSpec as P

GN_GROUPS = 32
HEIGHT = 48
WIDTH = 32
PIXELS = HEIGHT * WIDTH
CHANS = 640
KROWS = 9 * CHANS
ROWS = KROWS // 8
SPAN = 3 * CHANS
PADDED = PIXELS + 2 * WIDTH
SCALE = KROWS ** (-0.5)
MIB = 1 << 20
CUTS = ((0, 384), (384, 256))


def send_inner(value, dy, dz):
    def place(i):
        return ((i // 4 + dy) % 2) * 4 + (i % 4 + dz) % 4

    return lax.ppermute(value, "inner", [(i, place(i)) for i in range(8)])


def from_partner(value, by):
    return lax.ppermute(value, "group", [(i, (i - by) % 16) for i in range(16)])


def block_at(dy, dz):
    me = lax.axis_index("inner")
    return ((me // 4 + dy) % 2) * 4 + (me % 4 + dz) % 4


NEAR = [(0, 0), (0, 1), (0, 3), (0, 2), (1, 0), (1, 1), (1, 3), (1, 2)]


def group_mean(sums):
    chans = lax.broadcasted_iota(jnp.int32, (CHANS, 128), 0)
    first = lax.broadcasted_iota(jnp.int32, (CHANS, 128), 1) * (CHANS // GN_GROUPS)
    member = jnp.where((chans >= first) & (chans < first + CHANS // GN_GROUPS), 1.0, 0.0)
    total = jnp.broadcast_to(jnp.sum(sums, axis=0, keepdims=True), (8, CHANS))
    grouped = lax.dot_general(
        total, member, (((1,), (0,)), ((), ())), precision=lax.Precision.HIGHEST,
        preferred_element_type=jnp.float32,
    ) * (1.0 / (PIXELS * (CHANS // GN_GROUPS)))
    return lax.dot_general(
        grouped, member, (((1,), (1,)), ((), ())), precision=lax.Precision.HIGHEST,
        preferred_element_type=jnp.float32,
    )[0:1]


def store_shifts(ref, row, value, order):
    place = lax.broadcasted_iota(jnp.int32, (WIDTH, CHANS), 0)
    before = jnp.where(place == 0, 0.0, pltpu.roll(value, 1, 0))
    after = jnp.where(place == WIDTH - 1, 0.0, pltpu.roll(value, WIDTH - 1, 0))
    parts = (before, value, after) if order else (after, value, before)
    rows = pl.ds(pl.multiple_of((row + 1) * WIDTH, WIDTH), WIDTH)
    for b in range(3):
        ref[rows, b * CHANS : (b + 1) * CHANS] = parts[b].astype(jnp.bfloat16)


def zero_ends(ref):
    blank = jnp.zeros((WIDTH, SPAN), jnp.bfloat16)
    ref[0:WIDTH, :] = blank
    ref[PADDED - WIDTH : PADDED, :] = blank


def norm_grad_kernel(
    lat, cot, gain, bias, spread_out, *rest
):
    outs, (taps, cots, turned, grads, sem_h, sem_g) = rest[:8], rest[8:]

    def row_of(ref, r):
        return ref[pl.ds(pl.multiple_of(r * WIDTH, WIDTH), WIDTH), :].astype(jnp.float32)

    def fold(value):
        return jnp.sum(value.reshape(WIDTH // 8, 8, CHANS), axis=0)

    zeros = jnp.zeros((8, CHANS), jnp.float32)
    center = group_mean(lax.fori_loop(0, HEIGHT, lambda r, s: s + fold(row_of(lat, r)), zeros))

    def squares(r, s):
        off = row_of(lat, r) - center
        return s + fold(off * off)

    var = group_mean(lax.fori_loop(0, HEIGHT, squares, zeros))
    slope = lax.rsqrt(var + 1e-05) * gain[...]
    shift = bias[...]
    zero_ends(taps)
    zero_ends(cots)

    @pl.loop(0, HEIGHT)
    def _(r):
        normed = (row_of(lat, r) - center) * slope + shift
        store_shifts(taps, r, normed / (1.0 + jnp.exp(-normed)), True)
        store_shifts(cots, r, row_of(cot, r), False)

    keep = pltpu.make_async_copy(taps, spread_out, sem_h)
    keep.start()

    for j in range(PIXELS // 128):
        turned[:, j * 128 : (j + 1) * 128] = taps[
            WIDTH + j * 128 : WIDTH + (j + 1) * 128, CHANS : 2 * CHANS
        ].T

    @pl.loop(0, 3)
    def _(a):
        start = pl.multiple_of((2 - a) * WIDTH, WIDTH)
        for first in range(0, SPAN, 256):
            wide = min(256, SPAN - first)
            found = SCALE * jnp.dot(
                turned[...], cots[pl.ds(start, PIXELS), first : first + wide],
                preferred_element_type=jnp.float32,
            )
            found = found.astype(jnp.bfloat16)
            for part in range(first, first + wide, 128):
                b, col = part // CHANS, part % CHANS
                rows = pl.ds(pl.multiple_of((a * 3 + b) * CHANS, CHANS), CHANS)
                grads[rows, col : col + 128] = found[:, part - first : part - first + 128]

    copies = []
    for j, (dy, dz) in enumerate(NEAR):
        rows = pl.ds(pl.multiple_of(block_at(dy, dz) * ROWS, ROWS), ROWS)
        copies.append(pltpu.make_async_copy(grads.at[rows], outs[j], sem_g.at[j]))
        copies[-1].start()
    for copy in copies:
        copy.wait()
    keep.wait()


def norm_grad(latents, cotangent, gain, bias):
    full = pl.BlockSpec(memory_space=pltpu.VMEM)
    hbm = pl.BlockSpec(memory_space=pl.ANY)
    return pl.pallas_call(
        norm_grad_kernel,
        out_shape=[jax.ShapeDtypeStruct((PADDED, SPAN), jnp.bfloat16)]
        + [jax.ShapeDtypeStruct((ROWS, CHANS), jnp.bfloat16)] * 8,
        in_specs=[full] * 4,
        out_specs=[hbm] * 9,
        scratch_shapes=[
            pltpu.VMEM((PADDED, SPAN), jnp.bfloat16),
            pltpu.VMEM((PADDED, SPAN), jnp.bfloat16),
            pltpu.VMEM((CHANS, PIXELS), jnp.bfloat16),
            pltpu.VMEM((KROWS, CHANS), jnp.bfloat16),
            pltpu.SemaphoreType.DMA,
            pltpu.SemaphoreType.DMA((8,)),
        ],
        compiler_params=pltpu.CompilerParams(vmem_limit_bytes=48 * MIB),
        cost_estimate=pl.CostEstimate(
            flops=2 * PIXELS * KROWS * CHANS, bytes_accessed=18 * MIB, transcendentals=PIXELS * CHANS
        ),
        name="norm_grad",
    )(latents, cotangent, gain[None], bias[None])


def conv_kernel(places, first, wide, taps_hbm, lat_hbm, *rest):
    pieces, (out, taps, lat, weights, sem_t, sem_w) = rest[: len(places)], rest[len(places) :]
    copies = []
    for j, (dy, dz, row, rows) in enumerate(places):
        to = pl.ds(pl.multiple_of(block_at(dy, dz) * ROWS + row, 16), rows)
        src = pieces[j]
        if src.shape[1] != wide:
            src = src.at[:, first : first + wide]
        copies.append(pltpu.make_async_copy(src, weights.at[to], sem_w.at[j]))
    copies.append(pltpu.make_async_copy(taps_hbm, taps, sem_t.at[0]))
    copies.append(pltpu.make_async_copy(lat_hbm.at[:, first : first + wide], lat, sem_t.at[1]))
    for copy in copies:
        copy.start()
    for copy in copies:
        copy.wait()

    tall = 512

    @pl.loop(0, PIXELS // tall)
    def _(m):
        for col in range(0, wide, 256):
            step = min(256, wide - col)
            total = jnp.zeros((tall, step), jnp.float32)
            for a in range(3):
                rows = pl.ds(pl.multiple_of(m * tall + a * WIDTH, WIDTH), tall)
                total += jnp.dot(
                    taps[rows, :], weights[a * SPAN : (a + 1) * SPAN, col : col + step],
                    preferred_element_type=jnp.float32,
                )
            rows = pl.ds(pl.multiple_of(m * tall, tall), tall)
            base = lat[rows, col : col + step].astype(jnp.float32)
            out[rows, col : col + step] = (base + SCALE * total).astype(jnp.bfloat16)


def conv(taps, latents, places, pieces, first, wide):
    hbm = pl.BlockSpec(memory_space=pl.ANY)
    return pl.pallas_call(
        partial(conv_kernel, places, first, wide),
        out_shape=jax.ShapeDtypeStruct((PIXELS, wide), jnp.bfloat16),
        in_specs=[hbm] * (2 + len(pieces)),
        out_specs=pl.BlockSpec(memory_space=pltpu.VMEM),
        scratch_shapes=[
            pltpu.VMEM((PADDED, SPAN), jnp.bfloat16),
            pltpu.VMEM((PIXELS, wide), jnp.bfloat16),
            pltpu.VMEM((KROWS, wide), jnp.bfloat16),
            pltpu.SemaphoreType.DMA((2,)),
            pltpu.SemaphoreType.DMA((len(pieces),)),
        ],
        compiler_params=pltpu.CompilerParams(vmem_limit_bytes=40 * MIB),
        cost_estimate=pl.CostEstimate(
            flops=2 * PIXELS * KROWS * wide, bytes_accessed=16 * MIB, transcendentals=0
        ),
        name="conv",
    )(taps, latents, *pieces)


def together(values, *others):
    return lax.optimization_barrier(tuple(values) + others)[: len(values)]


def add(*values):
    return sum(v.astype(jnp.float32) for v in values).astype(jnp.bfloat16)


def whole(latents, cotangent, gain, bias, own_weight, own_moment, by):
    half = 352
    own = own_weight.astype(jnp.bfloat16)
    w_y = send_inner(own, 1, 0)
    w_m = send_inner(own, 0, 1)
    w_p = send_inner(own, 0, -1)
    w_partner = from_partner(own, by)
    latents, cotangent = together((latents, cotangent), own)
    taps, g00, g0p, g0m, g02, g10, g1p, g1m, g12 = norm_grad(latents, cotangent, gain, bias)
    g12, g1p, g1m = together((g12, g1p, g1m), w_y, w_m, w_p)
    a_y = send_inner(g12, 1, 0)
    a_p = send_inner(g1p, 0, 1)
    a_m = send_inner(g1m, 0, -1)
    far = add(a_y, g02)
    near = add(a_p, a_m, g10)
    far, near, w_m, w_p = together((far, near, w_m, w_p))
    b_up = send_inner(far[:half], 0, 1)
    b_dn = send_inner(far[half:], 0, -1)
    b_y = send_inner(near, 1, 0)
    top = send_inner(w_m[:half], 0, 1)
    bottom = send_inner(w_p[half:], 0, -1)
    to_up = jnp.concatenate([add(b_up, g0p[:half]), g0p[half:]])
    to_dn = jnp.concatenate([g0m[:half], add(b_dn, g0m[half:])])
    to_up, to_dn, top, bottom, b_y, w_partner = together((to_up, to_dn, top, bottom, b_y, w_partner))
    c_up = send_inner(to_up, 0, 1)
    c_dn = send_inner(to_dn, 0, -1)
    y_top = send_inner(top, 1, 0)
    y_bottom = send_inner(bottom, 1, 0)
    grad = (
        g00.astype(jnp.float32) + b_y.astype(jnp.float32)
        + c_up.astype(jnp.float32) + c_dn.astype(jnp.float32)
    )
    moved = 0.9 * own_moment + grad
    w_y, moved, y_top, y_bottom = together((w_y, moved, y_top, y_bottom))
    sent = []
    for first, wide in CUTS:
        y_m = send_inner(w_y[:, first : first + wide], 0, 1)
        y_p = send_inner(w_y[:, first : first + wide], 0, -1)
        sent.append((y_m, y_p))
    partner = from_partner(moved.astype(jnp.bfloat16), by).astype(jnp.float32)
    both = moved + partner
    new_moment = 0.5 * both
    new_weight = 0.5 * (own_weight + w_partner.astype(jnp.float32)) - 0.025 * both
    places = [
        (0, 0, 0, ROWS), (1, 0, 0, ROWS), (0, 3, 0, ROWS), (0, 1, 0, ROWS),
        (0, 2, 0, half), (0, 2, half, ROWS - half),
        (1, 2, 0, half), (1, 2, half, ROWS - half), (1, 3, 0, ROWS), (1, 1, 0, ROWS),
    ]
    parts = []
    ready = (own, w_y, w_m, w_p, top, bottom, y_top, y_bottom)
    for (first, wide), found in zip(CUTS, sent):
        parts.append(conv(taps, latents, places, ready + found, first, wide))
    return jnp.concatenate(parts, axis=1), new_weight, new_moment


def on_device(latents, cotangent, gain, bias, weight, momentum, step):
    branches = [partial(whole, by=1 << level) for level in range(4)]
    block_out, new_weight, new_moment = lax.switch(
        step[0] % 4, branches, latents[0], cotangent[0], gain, bias, weight[0], momentum[0]
    )
    return (block_out[None], new_weight[None], new_moment[None])


def solution(mesh):
    placed = (
        P(("group", "inner"), None, None),
        P(("group", "inner"), None, None),
        P(),
        P(),
        P("group", "inner", None),
        P("group", "inner", None),
        P(),
    )
    return jax.shard_map(
        on_device,
        mesh=mesh,
        in_specs=placed,
        out_specs=(
            P(("group", "inner"), None, None),
            P("group", "inner", None),
            P("group", "inner", None),
        ),
        check_vma=False,
    )
```

```python
from functools import partial

import jax
import jax.numpy as jnp
from jax import lax
from jax.experimental import pallas as pl
from jax.experimental.pallas import tpu as pltpu
from jax.sharding import PartitionSpec as P

GN_GROUPS = 32
HEIGHT = 48
WIDTH = 32
PIXELS = HEIGHT * WIDTH
CHANS = 640
KROWS = 9 * CHANS
ROWS = KROWS // 8
SPAN = 3 * CHANS
HALF = 352
PADDED = PIXELS + 2 * WIDTH
SCALE = KROWS ** (-0.5)
MIB = 1 << 20


def send_inner(value, dy, dz):
    def place(i):
        return ((i // 4 + dy) % 2) * 4 + (i % 4 + dz) % 4

    return lax.ppermute(value, "inner", [(i, place(i)) for i in range(8)])


def from_partner(value, by):
    return lax.ppermute(value, "group", [(i, (i - by) % 16) for i in range(16)])


def weight_from_partner(own, other, by):
    group = lax.axis_index("group")
    value = jnp.where(group // 8 != ((group - by) % 16) // 8, other, own)
    pairs = []
    for i in range(16):
        to = (i - by) % 16
        for j in range(8):
            pairs.append((i * 8 + j, to * 8 + (j if i // 8 == to // 8 else (j + 4) % 8)))
    return lax.ppermute(value, ("group", "inner"), pairs)


def block_at(dy, dz):
    me = lax.axis_index("inner")
    return ((me // 4 + dy) % 2) * 4 + (me % 4 + dz) % 4


NEAR = [(0, 0), (0, 1), (0, 3), (0, 2), (1, 0), (1, 1), (1, 3), (1, 2)]


def group_mean(sums):
    chans = lax.broadcasted_iota(jnp.int32, (CHANS, 128), 0)
    first = lax.broadcasted_iota(jnp.int32, (CHANS, 128), 1) * (CHANS // GN_GROUPS)
    member = jnp.where((chans >= first) & (chans < first + CHANS // GN_GROUPS), 1.0, 0.0)
    total = jnp.broadcast_to(jnp.sum(sums, axis=0, keepdims=True), (8, CHANS))
    grouped = lax.dot_general(
        total, member, (((1,), (0,)), ((), ())), precision=lax.Precision.HIGHEST,
        preferred_element_type=jnp.float32,
    ) * (1.0 / (PIXELS * (CHANS // GN_GROUPS)))
    return lax.dot_general(
        grouped, member, (((1,), (1,)), ((), ())), precision=lax.Precision.HIGHEST,
        preferred_element_type=jnp.float32,
    )[0:1]


def shifted(value):
    place = lax.broadcasted_iota(jnp.int32, (WIDTH, CHANS), 0)
    before = jnp.where(place == 0, 0.0, pltpu.roll(value, 1, 0))
    after = jnp.where(place == WIDTH - 1, 0.0, pltpu.roll(value, WIDTH - 1, 0))
    return before, value, after


def row_at(r):
    return pl.ds(pl.multiple_of(r * WIDTH, WIDTH), WIDTH)


def spread_rows(src, ref, turn):
    blank = jnp.zeros((WIDTH, SPAN), jnp.bfloat16)
    ref[0:WIDTH, :] = blank
    ref[PADDED - WIDTH : PADDED, :] = blank

    @pl.loop(0, HEIGHT, unroll=4)
    def _(r):
        parts = shifted(src[row_at(r), :].astype(jnp.float32))
        for b in range(3):
            part = parts[2 - b if turn else b]
            ref[row_at(r + 1), b * CHANS : (b + 1) * CHANS] = part.astype(jnp.bfloat16)


def grad_half(dy, turned, cots, grads, outs, sem):
    half = block_at(dy, 0) // 4
    first = half * 4

    def place(q):
        tap = q // 5
        return tap, pl.multiple_of((q - tap * 5) * 128, 128)

    def load(q):
        tap, col = place(q)
        a = (first + tap) // 3
        b = first + tap - 3 * a
        rows = pl.ds(pl.multiple_of((2 - a) * WIDTH, WIDTH), PIXELS)
        return cots[rows, pl.ds(pl.multiple_of(b * CHANS + col, 128), 128)]

    def tile(q, wide):
        right = jnp.concatenate([load(q + i) for i in range(wide)], axis=1)
        found = SCALE * jnp.dot(turned[...], right, preferred_element_type=jnp.float32)
        found = found.astype(jnp.bfloat16)
        for i in range(wide):
            tap, col = place(q + i)
            rows = pl.ds(pl.multiple_of(tap * CHANS, CHANS), CHANS)
            grads[rows, pl.ds(col, 128)] = found[:, i * 128 : (i + 1) * 128]

    @pl.loop(0, 24 // TILE)
    def _(j):
        tile(TILE * j, TILE)

    tile(24, 1)
    copies = []
    for j, dz in enumerate((0, 1, 3, 2)):
        begin = half * (4 * ROWS - 4 * CHANS) + (block_at(0, dz) % 4) * ROWS
        rows = pl.ds(pl.multiple_of(begin, 16), ROWS)
        copies.append(pltpu.make_async_copy(grads.at[rows], outs[j], sem.at[j]))
        copies[-1].start()
    for copy in copies:
        copy.wait()


def norm_grad_kernel(lat, cot, gain, bias, hidden_out, turned_out, *rest):
    outs, (hidden, turned, cots, grads, sem, sem_out) = rest[:4], rest[4:]

    def chunk_at(r):
        return pl.ds(pl.multiple_of(r * CHUNK, CHUNK), CHUNK)

    def chunk_of(r):
        return lat[chunk_at(r), :].astype(jnp.float32)

    def fold(value):
        return jnp.sum(value.reshape(CHUNK // 8, 8, CHANS), axis=0)

    chunks = PIXELS // CHUNK
    zeros = jnp.zeros((8, CHANS), jnp.float32)
    center = group_mean(lax.fori_loop(0, chunks, lambda r, s: s + fold(chunk_of(r)), zeros))

    def squares(r, s):
        off = chunk_of(r) - center
        return s + fold(off * off)

    var = group_mean(lax.fori_loop(0, chunks, squares, zeros))
    slope = lax.rsqrt(var + 1e-05) * gain[...]
    shift = bias[...]

    @pl.loop(0, chunks)
    def _(r):
        halved = 0.5 * ((chunk_of(r) - center) * slope + shift)
        rounded = (halved + halved * jnp.tanh(halved)).astype(jnp.bfloat16)
        hidden[chunk_at(r), :] = rounded
        turned[:, chunk_at(r)] = rounded.T

    spread_rows(cot, cots, True)
    keep = [
        pltpu.make_async_copy(hidden, hidden_out, sem_out.at[0]),
        pltpu.make_async_copy(turned, turned_out, sem_out.at[1]),
    ]
    for copy in keep:
        copy.start()
    grad_half(1, turned, cots, grads, outs, sem)
    for copy in keep:
        copy.wait()


def rest_grad_kernel(turned, cot, *rest):
    outs, (cots, grads, sem) = rest[:4], rest[4:]
    spread_rows(cot, cots, True)
    grad_half(0, turned, cots, grads, outs, sem)


def spread_kernel(hidden, taps):
    spread_rows(hidden, taps, False)


GRAD_SCRATCH = [
    pltpu.VMEM((PADDED, SPAN), jnp.bfloat16),
    pltpu.VMEM((5 * CHANS, CHANS), jnp.bfloat16),
    pltpu.SemaphoreType.DMA((4,)),
]
TILE = 6
WINDOW = 7 * 128
TALL = 512
STEPS = PIXELS // TALL
CHUNK = 128
SHORT = pl.CostEstimate(flops=10**6, bytes_accessed=10**5, transcendentals=0)
IN_VMEM = pl.BlockSpec(memory_space=pltpu.VMEM)
IN_ANY = pl.BlockSpec(memory_space=pl.ANY)


def norm_grad(latents, cotangent, gain, bias):
    return pl.pallas_call(
        norm_grad_kernel,
        out_shape=[
            jax.ShapeDtypeStruct((PIXELS, CHANS), jnp.bfloat16),
            jax.ShapeDtypeStruct((CHANS, PIXELS), jnp.bfloat16),
        ] + [jax.ShapeDtypeStruct((ROWS, CHANS), jnp.bfloat16)] * 4,
        in_specs=[IN_VMEM] * 4,
        out_specs=[IN_ANY] * 6,
        scratch_shapes=[
            pltpu.VMEM((PIXELS, CHANS), jnp.bfloat16),
            pltpu.VMEM((CHANS, PIXELS), jnp.bfloat16),
        ] + GRAD_SCRATCH + [pltpu.SemaphoreType.DMA((2,))],
        compiler_params=pltpu.CompilerParams(vmem_limit_bytes=58 * MIB),
        cost_estimate=SHORT,
        name="norm_grad",
    )(latents, cotangent, gain[None], bias[None])


def rest_grad(turned, cotangent):
    return pl.pallas_call(
        rest_grad_kernel,
        out_shape=[jax.ShapeDtypeStruct((ROWS, CHANS), jnp.bfloat16)] * 4,
        in_specs=[IN_VMEM] * 2,
        out_specs=[IN_ANY] * 4,
        scratch_shapes=GRAD_SCRATCH,
        compiler_params=pltpu.CompilerParams(vmem_limit_bytes=58 * MIB),
        cost_estimate=SHORT,
        name="rest_grad",
    )(turned, cotangent)


def spread(hidden):
    return pl.pallas_call(
        spread_kernel,
        out_shape=jax.ShapeDtypeStruct((PADDED, SPAN), jnp.bfloat16),
        in_specs=[IN_VMEM],
        out_specs=IN_VMEM,
        compiler_params=pltpu.CompilerParams(vmem_limit_bytes=20 * MIB),
        cost_estimate=SHORT,
        name="spread",
    )(hidden)


def conv_kernel(places, last, *refs):
    count = len(places)
    taps_hbm, pieces, refs = refs[0], refs[1 : 1 + count], refs[1 + count :]
    before_hbm = lat_hbm = None
    if last:
        before_hbm, lat_hbm, refs = refs[0], refs[1], refs[2:]
    out_hbm, taps, weights, before, lat, out, sem_w, sem_in, sem_out = refs

    def rows_of(m):
        return pl.ds(pl.multiple_of(m * TALL, TALL), TALL)

    def inputs(m):
        rows = pl.ds(pl.multiple_of(m * TALL + 2 * WIDTH, 2 * WIDTH), TALL)
        found = [pltpu.make_async_copy(taps_hbm.at[rows], taps.at[rows], sem_in.at[3 * m])]
        if last:
            rows = rows_of(m)
            found.append(pltpu.make_async_copy(before_hbm.at[rows], before.at[rows], sem_in.at[3 * m + 1]))
            found.append(pltpu.make_async_copy(lat_hbm.at[rows], lat.at[rows], sem_in.at[3 * m + 2]))
        return found

    def result(m):
        return pltpu.make_async_copy(out.at[rows_of(m)], out_hbm.at[rows_of(m)], sem_out.at[m])

    weights[...] = jnp.zeros_like(weights)
    head = pl.ds(0, 2 * WIDTH)
    copies = [pltpu.make_async_copy(taps_hbm.at[head], taps.at[head], sem_in.at[3 * STEPS])]
    copies[0].start()
    tiles = []
    blocks = list(dict.fromkeys(place[:2] for place in places))
    for j, (dy, dz, row, rows) in enumerate(places):
        block = block_at(dy, dz)
        base = block * ROWS // 128
        slot = blocks.index((dy, dz)) * WINDOW
        to = pl.ds(pl.multiple_of(slot + block * ROWS - base * 128 + row, 16), rows)
        copies.append(pltpu.make_async_copy(pieces[j], weights.at[to], sem_w.at[j]))
        copies[-1].start()
        if row == 0:
            for k in range(WINDOW // 128):
                tile = jnp.minimum(base + k, KROWS // 128 - 1)
                a = tile // (SPAN // 128)
                tiles.append((a * WIDTH, pl.multiple_of(tile * 128 - a * SPAN, 128)))
    for copy in inputs(0):
        copy.start()
    for copy in copies + inputs(0):
        copy.wait()
    for m in range(1, STEPS):
        for copy in inputs(m):
            copy.start()

    @pl.loop(0, STEPS)
    def _(m):
        @pl.when(m > 0)
        def _():
            for copy in inputs(m):
                copy.wait()

        left = jnp.concatenate([
            taps[pl.ds(pl.multiple_of(m * TALL + down, WIDTH), TALL), pl.ds(lane, 128)]
            for down, lane in tiles
        ], axis=1)
        total = jnp.dot(left, weights[...], preferred_element_type=jnp.float32)
        if last:
            total += before[rows_of(m), :].astype(jnp.float32)
            total = lat[rows_of(m), :].astype(jnp.float32) + SCALE * total
        out[rows_of(m), :] = total.astype(jnp.bfloat16)
        result(m).start()

    for m in range(STEPS):
        result(m).wait()


def conv(taps, places, pieces, others=()):
    blocks = len(set(place[:2] for place in places))
    return pl.pallas_call(
        partial(conv_kernel, places, len(others) > 0),
        out_shape=jax.ShapeDtypeStruct((PIXELS, CHANS), jnp.bfloat16),
        in_specs=[IN_ANY] * (1 + len(pieces) + len(others)),
        out_specs=IN_ANY,
        scratch_shapes=[
            pltpu.VMEM((PADDED, SPAN), jnp.bfloat16),
            pltpu.VMEM((blocks * WINDOW, CHANS), jnp.bfloat16),
            pltpu.VMEM((PIXELS, CHANS), jnp.bfloat16),
            pltpu.VMEM((PIXELS, CHANS), jnp.bfloat16),
            pltpu.VMEM((PIXELS, CHANS), jnp.bfloat16),
            pltpu.SemaphoreType.DMA((len(pieces),)),
            pltpu.SemaphoreType.DMA((3 * STEPS + 1,)),
            pltpu.SemaphoreType.DMA((STEPS,)),
        ],
        compiler_params=pltpu.CompilerParams(vmem_limit_bytes=58 * MIB),
        cost_estimate=SHORT,
        name="conv",
    )(taps, *pieces, *others)


def together(values, *others):
    return lax.optimization_barrier(tuple(values) + others)[: len(values)]


def add(*values):
    return sum(v.astype(jnp.float32) for v in values).astype(jnp.bfloat16)


def from_switch(step, branch, *state):
    return lax.switch(step[0] % 4, [partial(branch, 1 << level) for level in range(4)], *state)


def partner_and_conv(by, own, other, taps, w_m, w_p, top, bottom):
    w_partner = weight_from_partner(own, other, by)
    places = [
        (0, 0, 0, ROWS), (1, 0, 0, ROWS), (0, 3, 0, ROWS), (0, 1, 0, ROWS),
        (0, 2, 0, HALF), (0, 2, HALF, ROWS - HALF),
    ]
    return w_partner, conv(taps, places, (own, other, w_m, w_p, top, bottom))


def sums_kernel(a_y, g02, a_p, a_m, g10, far_top, far_bottom, near):
    def add(rows, *refs):
        return sum(ref[rows, :].astype(jnp.float32) for ref in refs).astype(jnp.bfloat16)

    far_top[...] = add(slice(0, HALF), a_y, g02)
    far_bottom[...] = add(slice(HALF, ROWS), a_y, g02)
    near[...] = add(slice(0, ROWS), a_p, a_m, g10)


def sums(*values):
    return pl.pallas_call(
        sums_kernel,
        out_shape=[jax.ShapeDtypeStruct((rows, CHANS), jnp.bfloat16) for rows in (HALF, ROWS - HALF, ROWS)],
        in_specs=[IN_VMEM] * 5,
        out_specs=[IN_VMEM] * 3,
        compiler_params=pltpu.CompilerParams(vmem_limit_bytes=20 * MIB),
        cost_estimate=SHORT,
        name="sums",
    )(*values)


def finish(by, moved, own_weight, w_partner):
    partner = from_partner(moved.astype(jnp.bfloat16), by).astype(jnp.float32)
    both = moved + partner
    new_moment = 0.5 * both
    new_weight = 0.5 * (own_weight + w_partner.astype(jnp.float32)) - 0.025 * both
    return new_weight, new_moment


def on_device(latents, cotangent, gain, bias, weight, momentum, step):
    latents, cotangent, own_weight, own_moment = latents[0], cotangent[0], weight[0], momentum[0]
    own = own_weight.astype(jnp.bfloat16)
    w_y = send_inner(own, 1, 0)
    w_m = send_inner(own, 0, 1)
    w_p = send_inner(own, 0, -1)
    latents, cotangent = together((latents, cotangent), own)
    hidden, turned, g10, g1p, g1m, g12 = norm_grad(latents, cotangent, gain, bias)
    g12, g1p, g1m, w_m, w_p, w_y = together((g12, g1p, g1m, w_m, w_p, w_y))
    a_y = send_inner(g12, 1, 0)
    a_p = send_inner(g1p, 0, 1)
    a_m = send_inner(g1m, 0, -1)
    top = send_inner(w_m[:HALF], 0, 1)
    bottom = send_inner(w_p[HALF:], 0, -1)
    g00, g0p, g0m, g02 = rest_grad(turned, cotangent)
    far_top, far_bottom, near = sums(a_y, g02, a_p, a_m, g10)
    b_up = send_inner(far_top, 0, 1)
    b_dn = send_inner(far_bottom, 0, -1)
    near, top, bottom, hidden = together((near, top, bottom, hidden))
    b_y = send_inner(near, 1, 0)
    corner = send_inner(jnp.concatenate([top, bottom]), 1, 0)
    taps = spread(hidden)
    b_up, b_dn, taps = together((b_up, b_dn, taps))
    to_up = jnp.concatenate([add(b_up, g0p[:HALF]), g0p[HALF:]])
    to_dn = jnp.concatenate([g0m[:HALF], add(b_dn, g0m[HALF:])])
    c_up = send_inner(to_up, 0, 1)
    c_dn = send_inner(to_dn, 0, -1)
    taps = together((taps,), to_up, to_dn)[0]
    w_partner, acc = from_switch(step, partner_and_conv, own, w_y, taps, w_m, w_p, top, bottom)
    w_y = together((w_y,), acc)[0]
    y_m = send_inner(w_y, 0, 1)
    y_p = send_inner(w_y, 0, -1)
    grad = (
        g00.astype(jnp.float32) + b_y.astype(jnp.float32)
        + c_up.astype(jnp.float32) + c_dn.astype(jnp.float32)
    )
    moved = 0.9 * own_moment + grad
    new_weight, new_moment = from_switch(step, finish, moved, own_weight, w_partner)
    y_m, y_p, corner = together((y_m, y_p, corner), new_weight, new_moment)
    places = [(1, 2, 0, ROWS), (1, 3, 0, ROWS), (1, 1, 0, ROWS)]
    block_out = conv(taps, places, (corner, y_m, y_p), (acc, latents))
    return (block_out[None], new_weight[None], new_moment[None])


def solution(mesh):
    placed = (
        P(("group", "inner"), None, None),
        P(("group", "inner"), None, None),
        P(),
        P(),
        P("group", "inner", None),
        P("group", "inner", None),
        P(),
    )
    return jax.shard_map(
        on_device,
        mesh=mesh,
        in_specs=placed,
        out_specs=(
            P(("group", "inner"), None, None),
            P("group", "inner", None),
            P("group", "inner", None),
        ),
        check_vma=False,
    )
```

```python
from functools import partial

import jax
import jax.numpy as jnp
from jax import lax
from jax.experimental import pallas as pl
from jax.experimental.pallas import tpu as pltpu
from jax.sharding import PartitionSpec as P

GN_GROUPS = 32
HEIGHT = 48
WIDTH = 32
PIXELS = HEIGHT * WIDTH
CHANS = 640
KROWS = 9 * CHANS
ROWS = KROWS // 8
SPAN = 3 * CHANS
HALF = 352
PADDED = PIXELS + 2 * WIDTH
SCALE = KROWS ** (-0.5)
MIB = 1 << 20


def send_inner(value, dy, dz):
    def place(i):
        return ((i // 4 + dy) % 2) * 4 + (i % 4 + dz) % 4

    return lax.ppermute(value, "inner", [(i, place(i)) for i in range(8)])


def from_partner(value, by):
    return lax.ppermute(value, "group", [(i, (i - by) % 16) for i in range(16)])


def to_send(own, other, step):
    group = lax.axis_index("group")
    by = jnp.left_shift(jnp.int32(1), step[0] % 4)
    return jnp.where(group // 8 != ((group - by) % 16) // 8, other, own)


def weight_from_partner(value, by):
    pairs = []
    for i in range(16):
        to = (i - by) % 16
        for j in range(8):
            pairs.append((i * 8 + j, to * 8 + (j if i // 8 == to // 8 else (j + 4) % 8)))
    return lax.ppermute(value, ("group", "inner"), pairs)


def block_at(dy, dz):
    me = lax.axis_index("inner")
    return ((me // 4 + dy) % 2) * 4 + (me % 4 + dz) % 4


NEAR = [(0, 0), (0, 1), (0, 3), (0, 2), (1, 0), (1, 1), (1, 3), (1, 2)]


def group_mean(sums):
    chans = lax.broadcasted_iota(jnp.int32, (CHANS, 128), 0)
    first = lax.broadcasted_iota(jnp.int32, (CHANS, 128), 1) * (CHANS // GN_GROUPS)
    member = jnp.where((chans >= first) & (chans < first + CHANS // GN_GROUPS), 1.0, 0.0)
    total = jnp.broadcast_to(jnp.sum(sums, axis=0, keepdims=True), (8, CHANS))
    grouped = lax.dot_general(
        total, member, (((1,), (0,)), ((), ())), precision=lax.Precision.HIGHEST,
        preferred_element_type=jnp.float32,
    ) * (1.0 / (PIXELS * (CHANS // GN_GROUPS)))
    return lax.dot_general(
        grouped, member, (((1,), (1,)), ((), ())), precision=lax.Precision.HIGHEST,
        preferred_element_type=jnp.float32,
    )[0:1]


def shifted(value):
    place = lax.broadcasted_iota(jnp.int32, (WIDTH, CHANS), 0)
    before = jnp.where(place == 0, 0.0, pltpu.roll(value, 1, 0))
    after = jnp.where(place == WIDTH - 1, 0.0, pltpu.roll(value, WIDTH - 1, 0))
    return before, value, after


def row_at(r):
    return pl.ds(pl.multiple_of(r * WIDTH, WIDTH), WIDTH)


def spread_rows(src, ref, turn):
    blank = jnp.zeros((WIDTH, SPAN), jnp.bfloat16)
    ref[0:WIDTH, :] = blank
    ref[PADDED - WIDTH : PADDED, :] = blank

    @pl.loop(0, HEIGHT, unroll=4)
    def _(r):
        parts = shifted(src[row_at(r), :].astype(jnp.float32))
        for b in range(3):
            part = parts[2 - b if turn else b]
            ref[row_at(r + 1), b * CHANS : (b + 1) * CHANS] = part.astype(jnp.bfloat16)


def grad_half(dy, turned, cots, grads, outs, sem):
    half = block_at(dy, 0) // 4
    first = half * 4

    def place(q):
        tap = q // 5
        return tap, pl.multiple_of((q - tap * 5) * 128, 128)

    def load(q):
        tap, col = place(q)
        a = (first + tap) // 3
        b = first + tap - 3 * a
        rows = pl.ds(pl.multiple_of((2 - a) * WIDTH, WIDTH), PIXELS)
        return cots[rows, pl.ds(pl.multiple_of(b * CHANS + col, 128), 128)]

    def tile(q, wide):
        right = jnp.concatenate([load(q + i) for i in range(wide)], axis=1)
        found = SCALE * jnp.dot(turned[...], right, preferred_element_type=jnp.float32)
        found = found.astype(jnp.bfloat16)
        for i in range(wide):
            tap, col = place(q + i)
            rows = pl.ds(pl.multiple_of(tap * CHANS, CHANS), CHANS)
            grads[rows, pl.ds(col, 128)] = found[:, i * 128 : (i + 1) * 128]

    @pl.loop(0, 24 // TILE)
    def _(j):
        tile(TILE * j, TILE)

    tile(24, 1)
    copies = []
    for j, dz in enumerate((0, 1, 3, 2)):
        begin = half * (4 * ROWS - 4 * CHANS) + (block_at(0, dz) % 4) * ROWS
        rows = pl.ds(pl.multiple_of(begin, 16), ROWS)
        copies.append(pltpu.make_async_copy(grads.at[rows], outs[j], sem.at[j]))
        copies[-1].start()
    for copy in copies:
        copy.wait()


def norm_grad_kernel(lat, cot, gain, bias, hidden_out, turned_out, *rest):
    outs, (hidden, turned, cots, grads, sem, sem_out) = rest[:4], rest[4:]

    def chunk_at(r):
        return pl.ds(pl.multiple_of(r * CHUNK, CHUNK), CHUNK)

    def chunk_of(r):
        return lat[chunk_at(r), :].astype(jnp.float32)

    def fold(value):
        return jnp.sum(value.reshape(CHUNK // 8, 8, CHANS), axis=0)

    chunks = PIXELS // CHUNK
    zeros = jnp.zeros((8, CHANS), jnp.float32)
    center = group_mean(lax.fori_loop(0, chunks, lambda r, s: s + fold(chunk_of(r)), zeros))

    def squares(r, s):
        off = chunk_of(r) - center
        return s + fold(off * off)

    var = group_mean(lax.fori_loop(0, chunks, squares, zeros))
    slope = lax.rsqrt(var + 1e-05) * gain[...]
    shift = bias[...]

    @pl.loop(0, chunks)
    def _(r):
        halved = 0.5 * ((chunk_of(r) - center) * slope + shift)
        rounded = (halved + halved * jnp.tanh(halved)).astype(jnp.bfloat16)
        hidden[chunk_at(r), :] = rounded
        turned[:, chunk_at(r)] = rounded.T

    spread_rows(cot, cots, True)
    keep = [
        pltpu.make_async_copy(hidden, hidden_out, sem_out.at[0]),
        pltpu.make_async_copy(turned, turned_out, sem_out.at[1]),
    ]
    for copy in keep:
        copy.start()
    grad_half(1, turned, cots, grads, outs, sem)
    for copy in keep:
        copy.wait()


def rest_grad_kernel(turned, cot, *rest):
    outs, (cots, grads, sem) = rest[:4], rest[4:]
    spread_rows(cot, cots, True)
    grad_half(0, turned, cots, grads, outs, sem)


def spread_kernel(hidden, taps):
    spread_rows(hidden, taps, False)


GRAD_SCRATCH = [
    pltpu.VMEM((PADDED, SPAN), jnp.bfloat16),
    pltpu.VMEM((5 * CHANS, CHANS), jnp.bfloat16),
    pltpu.SemaphoreType.DMA((4,)),
]
TILE = 6
WINDOW = 7 * 128
CHUNK = 128
SHORT = pl.CostEstimate(flops=10**6, bytes_accessed=10**5, transcendentals=0)
IN_VMEM = pl.BlockSpec(memory_space=pltpu.VMEM)
IN_ANY = pl.BlockSpec(memory_space=pl.ANY)


def norm_grad(latents, cotangent, gain, bias):
    return pl.pallas_call(
        norm_grad_kernel,
        out_shape=[
            jax.ShapeDtypeStruct((PIXELS, CHANS), jnp.bfloat16),
            jax.ShapeDtypeStruct((CHANS, PIXELS), jnp.bfloat16),
        ] + [jax.ShapeDtypeStruct((ROWS, CHANS), jnp.bfloat16)] * 4,
        in_specs=[IN_VMEM] * 4,
        out_specs=[IN_ANY] * 6,
        scratch_shapes=[
            pltpu.VMEM((PIXELS, CHANS), jnp.bfloat16),
            pltpu.VMEM((CHANS, PIXELS), jnp.bfloat16),
        ] + GRAD_SCRATCH + [pltpu.SemaphoreType.DMA((2,))],
        compiler_params=pltpu.CompilerParams(vmem_limit_bytes=58 * MIB),
        cost_estimate=SHORT,
        name="norm_grad",
    )(latents, cotangent, gain[None], bias[None])


def rest_grad(turned, cotangent):
    return pl.pallas_call(
        rest_grad_kernel,
        out_shape=[jax.ShapeDtypeStruct((ROWS, CHANS), jnp.bfloat16)] * 4,
        in_specs=[IN_VMEM] * 2,
        out_specs=[IN_ANY] * 4,
        scratch_shapes=GRAD_SCRATCH,
        compiler_params=pltpu.CompilerParams(vmem_limit_bytes=58 * MIB),
        cost_estimate=SHORT,
        name="rest_grad",
    )(turned, cotangent)


def spread(hidden):
    return pl.pallas_call(
        spread_kernel,
        out_shape=jax.ShapeDtypeStruct((PADDED, SPAN), jnp.bfloat16),
        in_specs=[IN_VMEM],
        out_specs=IN_VMEM,
        compiler_params=pltpu.CompilerParams(vmem_limit_bytes=20 * MIB),
        cost_estimate=SHORT,
        name="spread",
    )(hidden)


def conv_kernel(places, added, tall, *refs):
    steps = PIXELS // tall
    count = len(places)
    taps_hbm, pieces, refs = refs[0], refs[1 : 1 + count], refs[1 + count :]
    before_hbm = lat_hbm = None
    last = added == 2
    if added:
        before_hbm, refs = refs[0], refs[1:]
    if last:
        lat_hbm, refs = refs[0], refs[1:]
    out_hbm, taps, weights, before, lat, out, sem_w, sem_in, sem_out = refs

    def rows_of(m):
        return pl.ds(pl.multiple_of(m * tall, tall), tall)

    def inputs(m):
        rows = pl.ds(pl.multiple_of(m * tall + 2 * WIDTH, 2 * WIDTH), tall)
        found = [pltpu.make_async_copy(taps_hbm.at[rows], taps.at[rows], sem_in.at[3 * m])]
        rows = rows_of(m)
        if added:
            found.append(pltpu.make_async_copy(before_hbm.at[rows], before.at[rows], sem_in.at[3 * m + 1]))
        if last:
            found.append(pltpu.make_async_copy(lat_hbm.at[rows], lat.at[rows], sem_in.at[3 * m + 2]))
        return found

    def result(m):
        return pltpu.make_async_copy(out.at[rows_of(m)], out_hbm.at[rows_of(m)], sem_out.at[m])

    weights[...] = jnp.zeros_like(weights)
    head = pl.ds(0, 2 * WIDTH)
    copies = [pltpu.make_async_copy(taps_hbm.at[head], taps.at[head], sem_in.at[3 * steps])]
    copies[0].start()
    tiles = []
    blocks = list(dict.fromkeys(place[:2] for place in places))
    for j, (dy, dz, row, rows) in enumerate(places):
        block = block_at(dy, dz)
        base = block * ROWS // 128
        slot = blocks.index((dy, dz)) * WINDOW
        to = pl.ds(pl.multiple_of(slot + block * ROWS - base * 128 + row, 16), rows)
        copies.append(pltpu.make_async_copy(pieces[j], weights.at[to], sem_w.at[j]))
        copies[-1].start()
        if row == 0:
            for k in range(WINDOW // 128):
                tile = jnp.minimum(base + k, KROWS // 128 - 1)
                a = tile // (SPAN // 128)
                tiles.append((a * WIDTH, pl.multiple_of(tile * 128 - a * SPAN, 128)))
    for copy in inputs(0):
        copy.start()
    for copy in copies + inputs(0):
        copy.wait()
    for m in range(1, steps):
        for copy in inputs(m):
            copy.start()

    @pl.loop(0, steps)
    def _(m):
        @pl.when(m > 0)
        def _():
            for copy in inputs(m):
                copy.wait()

        left = jnp.concatenate([
            taps[pl.ds(pl.multiple_of(m * tall + down, WIDTH), tall), pl.ds(lane, 128)]
            for down, lane in tiles
        ], axis=1)
        total = jnp.dot(left, weights[...], preferred_element_type=jnp.float32)
        if added:
            total += before[rows_of(m), :].astype(jnp.float32)
        if last:
            total = lat[rows_of(m), :].astype(jnp.float32) + SCALE * total
        out[rows_of(m), :] = total.astype(jnp.bfloat16)
        result(m).start()

    for m in range(steps):
        result(m).wait()


def conv(taps, places, pieces, others=()):
    blocks = len(set(place[:2] for place in places))
    tall = 256 if blocks > 2 else 512
    return pl.pallas_call(
        partial(conv_kernel, places, len(others), tall),
        out_shape=jax.ShapeDtypeStruct((PIXELS, CHANS), jnp.bfloat16),
        in_specs=[IN_ANY] * (1 + len(pieces) + len(others)),
        out_specs=IN_ANY,
        scratch_shapes=[
            pltpu.VMEM((PADDED, SPAN), jnp.bfloat16),
            pltpu.VMEM((blocks * WINDOW, CHANS), jnp.bfloat16),
            pltpu.VMEM((PIXELS, CHANS), jnp.bfloat16),
            pltpu.VMEM((PIXELS, CHANS), jnp.bfloat16),
            pltpu.VMEM((PIXELS, CHANS), jnp.bfloat16),
            pltpu.SemaphoreType.DMA((len(pieces),)),
            pltpu.SemaphoreType.DMA((3 * (PIXELS // tall) + 1,)),
            pltpu.SemaphoreType.DMA((PIXELS // tall,)),
        ],
        compiler_params=pltpu.CompilerParams(vmem_limit_bytes=58 * MIB),
        cost_estimate=SHORT,
        name="conv",
    )(taps, *pieces, *others)


def together(values, *others):
    return lax.optimization_barrier(tuple(values) + others)[: len(values)]


def from_switch(step, branch, *state):
    return lax.switch(step[0] % 4, [partial(branch, 1 << level) for level in range(4)], *state)


def partner_and_conv(by, chosen, own, other, taps, w_m, w_p, top, bottom):
    w_partner = weight_from_partner(chosen, by)
    places = [
        (0, 0, 0, ROWS), (1, 0, 0, ROWS), (0, 3, 0, ROWS), (0, 1, 0, ROWS),
        (0, 2, 0, HALF), (0, 2, HALF, ROWS - HALF),
    ]
    return w_partner, conv(taps, places, (own, other, w_m, w_p, top, bottom))


def added(rows, *refs):
    return sum(ref[rows, :].astype(jnp.float32) for ref in refs).astype(jnp.bfloat16)


def sums_kernel(a_y, g02, a_p, a_m, g10, w_m, w_p, far_top, far_bottom, near, w_top, w_bottom):
    far_top[...] = added(slice(0, HALF), a_y, g02)
    far_bottom[...] = added(slice(HALF, ROWS), a_y, g02)
    near[...] = added(slice(0, ROWS), a_p, a_m, g10)
    w_top[...] = w_m[0:HALF, :]
    w_bottom[...] = w_p[HALF:ROWS, :]


def ends_kernel(b_up, g0p, b_dn, g0m, to_up, to_dn):
    to_up[0:HALF, :] = added(slice(0, HALF), b_up, g0p)
    to_up[HALF:ROWS, :] = g0p[HALF:ROWS, :]
    to_dn[0:HALF, :] = g0m[0:HALF, :]
    lower = b_dn[...].astype(jnp.float32) + g0m[HALF:ROWS, :].astype(jnp.float32)
    to_dn[HALF:ROWS, :] = lower.astype(jnp.bfloat16)


def small(kernel, name, rows, *values):
    return pl.pallas_call(
        kernel,
        out_shape=[jax.ShapeDtypeStruct((count, CHANS), jnp.bfloat16) for count in rows],
        in_specs=[IN_VMEM] * len(values),
        out_specs=[IN_VMEM] * len(rows),
        compiler_params=pltpu.CompilerParams(vmem_limit_bytes=20 * MIB),
        cost_estimate=SHORT,
        name=name,
    )(*values)


def moved_kernel(moment, g00, b_y, c_up, c_dn, moved, rounded):
    grad = sum(ref[...].astype(jnp.float32) for ref in (g00, b_y, c_up, c_dn))
    value = 0.9 * moment[...] + grad
    moved[...] = value
    rounded[...] = value.astype(jnp.bfloat16)


def moved_rows(*values):
    rows = pl.BlockSpec((ROWS // 3, CHANS), lambda i: (i, 0))
    return pl.pallas_call(
        moved_kernel,
        out_shape=[jax.ShapeDtypeStruct((ROWS, CHANS), kind) for kind in (jnp.float32, jnp.bfloat16)],
        grid=(3,),
        in_specs=[rows] * 5,
        out_specs=[rows] * 2,
        compiler_params=pltpu.CompilerParams(vmem_limit_bytes=20 * MIB),
        cost_estimate=SHORT,
        name="moved",
    )(*values)


def finish(by, rounded, moved, own_weight, w_partner, taps, corner, acc):
    partner = from_partner(rounded, by).astype(jnp.float32)
    both = moved + partner
    new_moment = 0.5 * both
    new_weight = 0.5 * (own_weight + w_partner.astype(jnp.float32)) - 0.025 * both
    return new_weight, new_moment, conv(taps, [(1, 2, 0, ROWS)], (corner,), (acc,))


def on_device(latents, cotangent, gain, bias, weight, momentum, step):
    latents, cotangent, own_weight, own_moment = latents[0], cotangent[0], weight[0], momentum[0]
    own = own_weight.astype(jnp.bfloat16)
    w_y = send_inner(own, 1, 0)
    w_m = send_inner(own, 0, 1)
    w_p = send_inner(own, 0, -1)
    latents, cotangent = together((latents, cotangent), own)
    hidden, turned, g10, g1p, g1m, g12 = norm_grad(latents, cotangent, gain, bias)
    g12, g1p, g1m, w_m, w_p, w_y = together((g12, g1p, g1m, w_m, w_p, w_y))
    a_y = send_inner(g12, 1, 0)
    a_p = send_inner(g1p, 0, 1)
    a_m = send_inner(g1m, 0, -1)
    g00, g0p, g0m, g02 = rest_grad(turned, cotangent)
    hidden = together((hidden,), g02)[0]
    taps = spread(hidden)
    a_y, a_p, a_m, taps = together((a_y, a_p, a_m, taps))
    far_top, far_bottom, near, w_top, w_bottom = small(
        sums_kernel, "sums", (HALF, ROWS - HALF, ROWS, HALF, ROWS - HALF),
        a_y, g02, a_p, a_m, g10, w_m, w_p,
    )
    b_up = send_inner(far_top, 0, 1)
    b_dn = send_inner(far_bottom, 0, -1)
    b_y = send_inner(near, 1, 0)
    top = send_inner(w_top, 0, 1)
    bottom = send_inner(w_bottom, 0, -1)
    own_late, w_y_late = together((own, w_y), far_top)
    chosen = to_send(own_late, w_y_late, step)
    b_up, b_dn, chosen = together((b_up, b_dn, chosen))
    to_up, to_dn = small(ends_kernel, "ends", (ROWS, ROWS), b_up, g0p, b_dn, g0m)
    c_up = send_inner(to_up, 0, 1)
    c_dn = send_inner(to_dn, 0, -1)
    taps, top, bottom, b_y = together((taps, top, bottom, b_y), to_up, to_dn)
    corner = send_inner(jnp.concatenate([top, bottom]), 1, 0)
    w_partner, acc = from_switch(
        step, partner_and_conv, chosen, own, w_y, taps, w_m, w_p, top, bottom
    )
    w_y = together((w_y,), acc)[0]
    y_m = send_inner(w_y, 0, 1)
    y_p = send_inner(w_y, 0, -1)
    moved, rounded = moved_rows(own_moment, g00, b_y, c_up, c_dn)
    new_weight, new_moment, acc = from_switch(
        step, finish, rounded, moved, own_weight, w_partner, taps, corner, acc
    )
    y_m, y_p = together((y_m, y_p), new_weight, new_moment)
    block_out = conv(taps, [(1, 3, 0, ROWS), (1, 1, 0, ROWS)], (y_m, y_p), (acc, latents))
    return (block_out[None], new_weight[None], new_moment[None])


def solution(mesh):
    placed = (
        P(("group", "inner"), None, None),
        P(("group", "inner"), None, None),
        P(),
        P(),
        P("group", "inner", None),
        P("group", "inner", None),
        P(),
    )
    return jax.shard_map(
        on_device,
        mesh=mesh,
        in_specs=placed,
        out_specs=(
            P(("group", "inner"), None, None),
            P("group", "inner", None),
            P("group", "inner", None),
        ),
        check_vma=False,
    )
```

```python
from functools import partial

import jax
import jax.numpy as jnp
from jax import lax
from jax.experimental import pallas as pl
from jax.experimental.pallas import tpu as pltpu
from jax.sharding import PartitionSpec as P

GN_GROUPS = 32
HEIGHT = 48
WIDTH = 32
PIXELS = HEIGHT * WIDTH
CHANS = 640
KROWS = 9 * CHANS
ROWS = KROWS // 8
SPAN = 3 * CHANS
HALF = 352
PADDED = PIXELS + 2 * WIDTH
SCALE = KROWS ** (-0.5)
MIB = 1 << 20


def send_inner(value, dy, dz):
    def place(i):
        return ((i // 4 + dy) % 2) * 4 + (i % 4 + dz) % 4

    return lax.ppermute(value, "inner", [(i, place(i)) for i in range(8)])


def from_partner(value, by):
    return lax.ppermute(value, "group", [(i, (i - by) % 16) for i in range(16)])


def to_send(own, other, step):
    group = lax.axis_index("group")
    by = jnp.left_shift(jnp.int32(1), step[0] % 4)
    return jnp.where(group // 8 != ((group - by) % 16) // 8, other, own)


def weight_from_partner(value, by):
    pairs = []
    for i in range(16):
        to = (i - by) % 16
        for j in range(8):
            pairs.append((i * 8 + j, to * 8 + (j if i // 8 == to // 8 else (j + 4) % 8)))
    return lax.ppermute(value, ("group", "inner"), pairs)


def block_at(dy, dz):
    me = lax.axis_index("inner")
    return ((me // 4 + dy) % 2) * 4 + (me % 4 + dz) % 4


NEAR = [(0, 0), (0, 1), (0, 3), (0, 2), (1, 0), (1, 1), (1, 3), (1, 2)]


def group_mean(sums):
    chans = lax.broadcasted_iota(jnp.int32, (CHANS, 128), 0)
    first = lax.broadcasted_iota(jnp.int32, (CHANS, 128), 1) * (CHANS // GN_GROUPS)
    member = jnp.where((chans >= first) & (chans < first + CHANS // GN_GROUPS), 1.0, 0.0)
    total = jnp.broadcast_to(jnp.sum(sums, axis=0, keepdims=True), (8, CHANS))
    grouped = lax.dot_general(
        total, member, (((1,), (0,)), ((), ())), precision=lax.Precision.HIGHEST,
        preferred_element_type=jnp.float32,
    ) * (1.0 / (PIXELS * (CHANS // GN_GROUPS)))
    return lax.dot_general(
        grouped, member, (((1,), (1,)), ((), ())), precision=lax.Precision.HIGHEST,
        preferred_element_type=jnp.float32,
    )[0:1]


def shifted(value):
    place = lax.broadcasted_iota(jnp.int32, (WIDTH, CHANS), 0)
    before = jnp.where(place == 0, 0.0, pltpu.roll(value, 1, 0))
    after = jnp.where(place == WIDTH - 1, 0.0, pltpu.roll(value, WIDTH - 1, 0))
    return before, value, after


def row_at(r):
    return pl.ds(pl.multiple_of(r * WIDTH, WIDTH), WIDTH)


def spread_rows(src, ref, turn):
    blank = jnp.zeros((WIDTH, SPAN), jnp.bfloat16)
    ref[0:WIDTH, :] = blank
    ref[PADDED - WIDTH : PADDED, :] = blank

    @pl.loop(0, HEIGHT, unroll=4)
    def _(r):
        parts = shifted(src[row_at(r), :].astype(jnp.float32))
        for b in range(3):
            part = parts[2 - b if turn else b]
            ref[row_at(r + 1), b * CHANS : (b + 1) * CHANS] = part.astype(jnp.bfloat16)


def grad_half(dy, turned, cots, grads, outs, sem):
    half = block_at(dy, 0) // 4
    first = half * 4

    def place(q):
        tap = q // 5
        return tap, pl.multiple_of((q - tap * 5) * 128, 128)

    def load(q):
        tap, col = place(q)
        a = (first + tap) // 3
        b = first + tap - 3 * a
        rows = pl.ds(pl.multiple_of((2 - a) * WIDTH, WIDTH), PIXELS)
        return cots[rows, pl.ds(pl.multiple_of(b * CHANS + col, 128), 128)]

    def tile(q, wide):
        right = jnp.concatenate([load(q + i) for i in range(wide)], axis=1)
        found = SCALE * jnp.dot(turned[...], right, preferred_element_type=jnp.float32)
        found = found.astype(jnp.bfloat16)
        for i in range(wide):
            tap, col = place(q + i)
            rows = pl.ds(pl.multiple_of(tap * CHANS, CHANS), CHANS)
            grads[rows, pl.ds(col, 128)] = found[:, i * 128 : (i + 1) * 128]

    @pl.loop(0, 24 // TILE)
    def _(j):
        tile(TILE * j, TILE)

    tile(24, 1)
    copies = []
    for j, dz in enumerate((0, 1, 3, 2)):
        begin = half * (4 * ROWS - 4 * CHANS) + (block_at(0, dz) % 4) * ROWS
        rows = pl.ds(pl.multiple_of(begin, 16), ROWS)
        copies.append(pltpu.make_async_copy(grads.at[rows], outs[j], sem.at[j]))
        copies[-1].start()
    for copy in copies:
        copy.wait()


def norm_grad_kernel(lat, cot, affine, hidden_out, turned_out, *rest):
    outs, (hidden, turned, cots, grads, sem, sem_out) = rest[:4], rest[4:]

    def chunk_at(r):
        return pl.ds(pl.multiple_of(r * CHUNK, CHUNK), CHUNK)

    def chunk_of(r):
        return lat[chunk_at(r), :].astype(jnp.float32)

    def fold(value):
        return jnp.sum(value.reshape(CHUNK // 8, 8, CHANS), axis=0)

    chunks = PIXELS // CHUNK
    zeros = jnp.zeros((8, CHANS), jnp.float32)
    center = group_mean(lax.fori_loop(0, chunks, lambda r, s: s + fold(chunk_of(r)), zeros))

    def squares(r, s):
        off = chunk_of(r) - center
        return s + fold(off * off)

    var = group_mean(lax.fori_loop(0, chunks, squares, zeros))
    slope = lax.rsqrt(var + 1e-05) * affine[0:1, :]
    shift = affine[1:2, :]

    @pl.loop(0, chunks)
    def _(r):
        halved = 0.5 * ((chunk_of(r) - center) * slope + shift)
        rounded = (halved + halved * jnp.tanh(halved)).astype(jnp.bfloat16)
        hidden[chunk_at(r), :] = rounded
        turned[:, chunk_at(r)] = rounded.T

    spread_rows(cot, cots, True)
    keep = [
        pltpu.make_async_copy(hidden, hidden_out, sem_out.at[0]),
        pltpu.make_async_copy(turned, turned_out, sem_out.at[1]),
    ]
    for copy in keep:
        copy.start()
    grad_half(1, turned, cots, grads, outs, sem)
    for copy in keep:
        copy.wait()


def rest_grad_kernel(turned, cot, *rest):
    outs, (cots, grads, sem) = rest[:4], rest[4:]
    spread_rows(cot, cots, True)
    grad_half(0, turned, cots, grads, outs, sem)


def spread_kernel(hidden, taps):
    spread_rows(hidden, taps, False)


GRAD_SCRATCH = [
    pltpu.VMEM((PADDED, SPAN), jnp.bfloat16),
    pltpu.VMEM((5 * CHANS, CHANS), jnp.bfloat16),
    pltpu.SemaphoreType.DMA((4,)),
]
TILE = 6
WINDOW = 7 * 128
CHUNK = 128
SHORT = pl.CostEstimate(flops=10**6, bytes_accessed=10**5, transcendentals=0)
IN_VMEM = pl.BlockSpec(memory_space=pltpu.VMEM)
IN_ANY = pl.BlockSpec(memory_space=pl.ANY)


def norm_grad(latents, cotangent, gain, bias):
    return pl.pallas_call(
        norm_grad_kernel,
        out_shape=[
            jax.ShapeDtypeStruct((PIXELS, CHANS), jnp.bfloat16),
            jax.ShapeDtypeStruct((CHANS, PIXELS), jnp.bfloat16),
        ] + [jax.ShapeDtypeStruct((ROWS, CHANS), jnp.bfloat16)] * 4,
        in_specs=[IN_VMEM] * 3,
        out_specs=[IN_ANY] * 6,
        scratch_shapes=[
            pltpu.VMEM((PIXELS, CHANS), jnp.bfloat16),
            pltpu.VMEM((CHANS, PIXELS), jnp.bfloat16),
        ] + GRAD_SCRATCH + [pltpu.SemaphoreType.DMA((2,))],
        compiler_params=pltpu.CompilerParams(vmem_limit_bytes=58 * MIB),
        cost_estimate=SHORT,
        name="norm_grad",
    )(latents, cotangent, jnp.stack([gain, bias]))


def rest_grad(turned, cotangent):
    return pl.pallas_call(
        rest_grad_kernel,
        out_shape=[jax.ShapeDtypeStruct((ROWS, CHANS), jnp.bfloat16)] * 4,
        in_specs=[IN_VMEM] * 2,
        out_specs=[IN_ANY] * 4,
        scratch_shapes=GRAD_SCRATCH,
        compiler_params=pltpu.CompilerParams(vmem_limit_bytes=58 * MIB),
        cost_estimate=SHORT,
        name="rest_grad",
    )(turned, cotangent)


def spread(hidden):
    return pl.pallas_call(
        spread_kernel,
        out_shape=jax.ShapeDtypeStruct((PADDED, SPAN), jnp.bfloat16),
        in_specs=[IN_VMEM],
        out_specs=IN_VMEM,
        compiler_params=pltpu.CompilerParams(vmem_limit_bytes=20 * MIB),
        cost_estimate=SHORT,
        name="spread",
    )(hidden)


def conv_kernel(places, added, tall, *refs):
    steps = PIXELS // tall
    count = len(places)
    taps_hbm, pieces, refs = refs[0], refs[1 : 1 + count], refs[1 + count :]
    before_hbm = lat_hbm = None
    last = added == 2
    if added:
        before_hbm, refs = refs[0], refs[1:]
    if last:
        lat_hbm, refs = refs[0], refs[1:]
    out_hbm, taps, weights, before, lat, out, sem_w, sem_in, sem_out = refs

    def rows_of(m):
        return pl.ds(pl.multiple_of(m * tall, tall), tall)

    def inputs(m):
        rows = pl.ds(pl.multiple_of(m * tall + 2 * WIDTH, 2 * WIDTH), tall)
        found = [pltpu.make_async_copy(taps_hbm.at[rows], taps.at[rows], sem_in.at[3 * m])]
        rows = rows_of(m)
        if added:
            found.append(pltpu.make_async_copy(before_hbm.at[rows], before.at[rows], sem_in.at[3 * m + 1]))
        if last:
            found.append(pltpu.make_async_copy(lat_hbm.at[rows], lat.at[rows], sem_in.at[3 * m + 2]))
        return found

    def result(m):
        return pltpu.make_async_copy(out.at[rows_of(m)], out_hbm.at[rows_of(m)], sem_out.at[m])

    weights[...] = jnp.zeros_like(weights)
    head = pl.ds(0, 2 * WIDTH)
    copies = [pltpu.make_async_copy(taps_hbm.at[head], taps.at[head], sem_in.at[3 * steps])]
    copies[0].start()
    tiles = []
    blocks = list(dict.fromkeys(place[:2] for place in places))
    for j, (dy, dz, row, rows) in enumerate(places):
        block = block_at(dy, dz)
        base = block * ROWS // 128
        slot = blocks.index((dy, dz)) * WINDOW
        to = pl.ds(pl.multiple_of(slot + block * ROWS - base * 128 + row, 16), rows)
        copies.append(pltpu.make_async_copy(pieces[j], weights.at[to], sem_w.at[j]))
        copies[-1].start()
        if row == 0:
            for k in range(WINDOW // 128):
                tile = jnp.minimum(base + k, KROWS // 128 - 1)
                a = tile // (SPAN // 128)
                tiles.append((a * WIDTH, pl.multiple_of(tile * 128 - a * SPAN, 128)))
    for copy in inputs(0):
        copy.start()
    for copy in copies + inputs(0):
        copy.wait()
    for m in range(1, steps):
        for copy in inputs(m):
            copy.start()

    @pl.loop(0, steps)
    def _(m):
        @pl.when(m > 0)
        def _():
            for copy in inputs(m):
                copy.wait()

        left = jnp.concatenate([
            taps[pl.ds(pl.multiple_of(m * tall + down, WIDTH), tall), pl.ds(lane, 128)]
            for down, lane in tiles
        ], axis=1)
        total = jnp.dot(left, weights[...], preferred_element_type=jnp.float32)
        if added:
            total += before[rows_of(m), :].astype(jnp.float32)
        if last:
            total = lat[rows_of(m), :].astype(jnp.float32) + SCALE * total
        out[rows_of(m), :] = total.astype(jnp.bfloat16)
        result(m).start()

    for m in range(steps):
        result(m).wait()


def conv(taps, places, pieces, others=(), tall=None):
    blocks = len(set(place[:2] for place in places))
    tall = tall or (256 if blocks > 2 else 512)
    return pl.pallas_call(
        partial(conv_kernel, places, len(others), tall),
        out_shape=jax.ShapeDtypeStruct((PIXELS, CHANS), jnp.bfloat16),
        in_specs=[IN_ANY] * (1 + len(pieces) + len(others)),
        out_specs=IN_ANY,
        scratch_shapes=[
            pltpu.VMEM((PADDED, SPAN), jnp.bfloat16),
            pltpu.VMEM((blocks * WINDOW, CHANS), jnp.bfloat16),
            pltpu.VMEM((PIXELS, CHANS), jnp.bfloat16),
            pltpu.VMEM((PIXELS, CHANS), jnp.bfloat16),
            pltpu.VMEM((PIXELS, CHANS), jnp.bfloat16),
            pltpu.SemaphoreType.DMA((len(pieces),)),
            pltpu.SemaphoreType.DMA((3 * (PIXELS // tall) + 1,)),
            pltpu.SemaphoreType.DMA((PIXELS // tall,)),
        ],
        compiler_params=pltpu.CompilerParams(vmem_limit_bytes=58 * MIB),
        cost_estimate=SHORT,
        name="conv",
    )(taps, *pieces, *others)


def together(values, *others):
    return lax.optimization_barrier(tuple(values) + others)[: len(values)]


def from_switch(step, branch, *state):
    return lax.switch(step[0] % 4, [partial(branch, 1 << level) for level in range(4)], *state)


def partner_and_conv(by, chosen, own, other, taps, w_m, w_p):
    w_partner = weight_from_partner(chosen, by)
    places = [(0, 0, 0, ROWS), (1, 0, 0, ROWS), (0, 3, 0, ROWS), (0, 1, 0, ROWS)]
    return w_partner, conv(taps, places, (own, other, w_m, w_p))


def join_kernel(top, bottom, both):
    both[0:HALF, :] = top[...]
    both[HALF:ROWS, :] = bottom[...]


def added(rows, *refs):
    return sum(ref[rows, :].astype(jnp.float32) for ref in refs).astype(jnp.bfloat16)


def sums_kernel(a_y, g02, a_p, a_m, g10, w_m, w_p, far_top, far_bottom, near, w_top, w_bottom):
    far_top[...] = added(slice(0, HALF), a_y, g02)
    far_bottom[...] = added(slice(HALF, ROWS), a_y, g02)
    near[...] = added(slice(0, ROWS), a_p, a_m, g10)
    w_top[...] = w_m[0:HALF, :]
    w_bottom[...] = w_p[HALF:ROWS, :]


def ends_kernel(b_up, g0p, b_dn, g0m, to_up, to_dn):
    to_up[0:HALF, :] = added(slice(0, HALF), b_up, g0p)
    to_up[HALF:ROWS, :] = g0p[HALF:ROWS, :]
    to_dn[0:HALF, :] = g0m[0:HALF, :]
    lower = b_dn[...].astype(jnp.float32) + g0m[HALF:ROWS, :].astype(jnp.float32)
    to_dn[HALF:ROWS, :] = lower.astype(jnp.bfloat16)


def small(kernel, name, rows, *values):
    return pl.pallas_call(
        kernel,
        out_shape=[jax.ShapeDtypeStruct((count, CHANS), jnp.bfloat16) for count in rows],
        in_specs=[IN_VMEM] * len(values),
        out_specs=[IN_VMEM] * len(rows),
        compiler_params=pltpu.CompilerParams(vmem_limit_bytes=20 * MIB),
        cost_estimate=SHORT,
        name=name,
    )(*values)


def moved_kernel(moment, g00, b_y, c_up, c_dn, moved, rounded):
    grad = sum(ref[...].astype(jnp.float32) for ref in (g00, b_y, c_up, c_dn))
    value = 0.9 * moment[...] + grad
    moved[...] = value
    rounded[...] = value.astype(jnp.bfloat16)


def moved_rows(*values):
    rows = pl.BlockSpec((ROWS // 3, CHANS), lambda i: (i, 0))
    return pl.pallas_call(
        moved_kernel,
        out_shape=[jax.ShapeDtypeStruct((ROWS, CHANS), kind) for kind in (jnp.float32, jnp.bfloat16)],
        grid=(3,),
        in_specs=[rows] * 5,
        out_specs=[rows] * 2,
        compiler_params=pltpu.CompilerParams(vmem_limit_bytes=20 * MIB),
        cost_estimate=SHORT,
        name="moved",
    )(*values)


def finish(by, rounded, moved, own_weight, w_partner, taps, w_far, corner, acc):
    partner = from_partner(rounded, by).astype(jnp.float32)
    both = moved + partner
    new_moment = 0.5 * both
    new_weight = 0.5 * (own_weight + w_partner.astype(jnp.float32)) - 0.025 * both
    return new_weight, new_moment, conv(
        taps, [(0, 2, 0, ROWS), (1, 2, 0, ROWS)], (w_far, corner), (acc,), 256
    )


def on_device(latents, cotangent, gain, bias, weight, momentum, step):
    latents, cotangent, own_weight, own_moment = latents[0], cotangent[0], weight[0], momentum[0]
    own = own_weight.astype(jnp.bfloat16)
    w_y = send_inner(own, 1, 0)
    w_m = send_inner(own, 0, 1)
    w_p = send_inner(own, 0, -1)
    latents, cotangent = together((latents, cotangent), own)
    hidden, turned, g10, g1p, g1m, g12 = norm_grad(latents, cotangent, gain, bias)
    g12, g1p, g1m, w_m, w_p, w_y = together((g12, g1p, g1m, w_m, w_p, w_y))
    a_y = send_inner(g12, 1, 0)
    a_p = send_inner(g1p, 0, 1)
    a_m = send_inner(g1m, 0, -1)
    g00, g0p, g0m, g02 = rest_grad(turned, cotangent)
    hidden = together((hidden,), g02)[0]
    taps = spread(hidden)
    a_y, a_p, a_m, taps = together((a_y, a_p, a_m, taps))
    far_top, far_bottom, near, w_top, w_bottom = small(
        sums_kernel, "sums", (HALF, ROWS - HALF, ROWS, HALF, ROWS - HALF),
        a_y, g02, a_p, a_m, g10, w_m, w_p,
    )
    b_up = send_inner(far_top, 0, 1)
    b_dn = send_inner(far_bottom, 0, -1)
    b_y = send_inner(near, 1, 0)
    top = send_inner(w_top, 0, 1)
    bottom = send_inner(w_bottom, 0, -1)
    own_late, w_y_late = together((own, w_y), far_top)
    chosen = to_send(own_late, w_y_late, step)
    b_up, b_dn, chosen = together((b_up, b_dn, chosen))
    to_up, to_dn = small(ends_kernel, "ends", (ROWS, ROWS), b_up, g0p, b_dn, g0m)
    c_up = send_inner(to_up, 0, 1)
    c_dn = send_inner(to_dn, 0, -1)
    taps, top, bottom, b_y = together((taps, top, bottom, b_y), to_up, to_dn)
    w_far, = small(join_kernel, "join", (ROWS,), top, bottom)
    corner = send_inner(w_far, 1, 0)
    w_partner, acc = from_switch(
        step, partner_and_conv, chosen, own, w_y, taps, w_m, w_p
    )
    w_y = together((w_y,), acc)[0]
    y_m = send_inner(w_y, 0, 1)
    y_p = send_inner(w_y, 0, -1)
    moved, rounded = moved_rows(own_moment, g00, b_y, c_up, c_dn)
    new_weight, new_moment, acc = from_switch(
        step, finish, rounded, moved, own_weight, w_partner, taps, w_far, corner, acc
    )
    y_m, y_p = together((y_m, y_p), new_weight, new_moment)
    block_out = conv(taps, [(1, 3, 0, ROWS), (1, 1, 0, ROWS)], (y_m, y_p), (acc, latents))
    return (block_out[None], new_weight[None], new_moment[None])


def solution(mesh):
    placed = (
        P(("group", "inner"), None, None),
        P(("group", "inner"), None, None),
        P(),
        P(),
        P("group", "inner", None),
        P("group", "inner", None),
        P(),
    )
    return jax.shard_map(
        on_device,
        mesh=mesh,
        in_specs=placed,
        out_specs=(
            P(("group", "inner"), None, None),
            P("group", "inner", None),
            P("group", "inner", None),
        ),
        check_vma=False,
    )
```

```python
from functools import partial

import jax
import jax.numpy as jnp
from jax import lax
from jax.experimental import pallas as pl
from jax.experimental.pallas import tpu as pltpu
from jax.sharding import PartitionSpec as P

GN_GROUPS = 32
HEIGHT = 48
WIDTH = 32
PIXELS = HEIGHT * WIDTH
CHANS = 640
KROWS = 9 * CHANS
ROWS = KROWS // 8
SPAN = 3 * CHANS
HALF = 352
PADDED = PIXELS + 2 * WIDTH
SCALE = KROWS ** (-0.5)
MIB = 1 << 20


def send_inner(value, dy, dz):
    def place(i):
        return ((i // 4 + dy) % 2) * 4 + (i % 4 + dz) % 4

    return lax.ppermute(value, "inner", [(i, place(i)) for i in range(8)])


def from_partner(value, by):
    return lax.ppermute(value, "group", [(i, (i - by) % 16) for i in range(16)])


def to_send(own, other, step):
    group = lax.axis_index("group")
    by = jnp.left_shift(jnp.int32(1), step[0] % 4)
    return jnp.where(group // 8 != ((group - by) % 16) // 8, other, own)


def weight_from_partner(value, by):
    pairs = []
    for i in range(16):
        to = (i - by) % 16
        for j in range(8):
            pairs.append((i * 8 + j, to * 8 + (j if i // 8 == to // 8 else (j + 4) % 8)))
    return lax.ppermute(value, ("group", "inner"), pairs)


def block_at(dy, dz):
    me = lax.axis_index("inner")
    return ((me // 4 + dy) % 2) * 4 + (me % 4 + dz) % 4


NEAR = [(0, 0), (0, 1), (0, 3), (0, 2), (1, 0), (1, 1), (1, 3), (1, 2)]


def group_mean(sums):
    chans = lax.broadcasted_iota(jnp.int32, (CHANS, 128), 0)
    first = lax.broadcasted_iota(jnp.int32, (CHANS, 128), 1) * (CHANS // GN_GROUPS)
    member = jnp.where((chans >= first) & (chans < first + CHANS // GN_GROUPS), 1.0, 0.0)
    total = jnp.broadcast_to(jnp.sum(sums, axis=0, keepdims=True), (8, CHANS))
    grouped = lax.dot_general(
        total, member, (((1,), (0,)), ((), ())), precision=lax.Precision.HIGHEST,
        preferred_element_type=jnp.float32,
    ) * (1.0 / (PIXELS * (CHANS // GN_GROUPS)))
    return lax.dot_general(
        grouped, member, (((1,), (1,)), ((), ())), precision=lax.Precision.HIGHEST,
        preferred_element_type=jnp.float32,
    )[0:1]


def shifted(value):
    place = lax.broadcasted_iota(jnp.int32, (WIDTH, CHANS), 0)
    before = jnp.where(place == 0, 0.0, pltpu.roll(value, 1, 0))
    after = jnp.where(place == WIDTH - 1, 0.0, pltpu.roll(value, WIDTH - 1, 0))
    return before, value, after


def row_at(r):
    return pl.ds(pl.multiple_of(r * WIDTH, WIDTH), WIDTH)


def spread_rows(src, ref, turn):
    blank = jnp.zeros((WIDTH, SPAN), jnp.bfloat16)
    ref[0:WIDTH, :] = blank
    ref[PADDED - WIDTH : PADDED, :] = blank

    @pl.loop(0, HEIGHT, unroll=4)
    def _(r):
        parts = shifted(src[row_at(r), :].astype(jnp.float32))
        for b in range(3):
            part = parts[2 - b if turn else b]
            ref[row_at(r + 1), b * CHANS : (b + 1) * CHANS] = part.astype(jnp.bfloat16)


def grad_half(dy, turned, cots, grads, outs, sem):
    half = block_at(dy, 0) // 4
    first = half * 4

    def place(q):
        tap = q // 5
        return tap, pl.multiple_of((q - tap * 5) * 128, 128)

    def load(q):
        tap, col = place(q)
        a = (first + tap) // 3
        b = first + tap - 3 * a
        rows = pl.ds(pl.multiple_of((2 - a) * WIDTH, WIDTH), PIXELS)
        return cots[rows, pl.ds(pl.multiple_of(b * CHANS + col, 128), 128)]

    def tile(q, wide):
        right = jnp.concatenate([load(q + i) for i in range(wide)], axis=1)
        found = SCALE * jnp.dot(turned[...], right, preferred_element_type=jnp.float32)
        found = found.astype(jnp.bfloat16)
        for i in range(wide):
            tap, col = place(q + i)
            rows = pl.ds(pl.multiple_of(tap * CHANS, CHANS), CHANS)
            grads[rows, pl.ds(col, 128)] = found[:, i * 128 : (i + 1) * 128]

    @pl.loop(0, 24 // TILE)
    def _(j):
        tile(TILE * j, TILE)

    tile(24, 1)
    copies = []
    for j, dz in enumerate((0, 1, 3, 2)):
        begin = half * (4 * ROWS - 4 * CHANS) + (block_at(0, dz) % 4) * ROWS
        rows = pl.ds(pl.multiple_of(begin, 16), ROWS)
        copies.append(pltpu.make_async_copy(grads.at[rows], outs[j], sem.at[j]))
        copies[-1].start()
    for copy in copies:
        copy.wait()


def norm_grad_kernel(lat, cot, affine, hidden_out, turned_out, *rest):
    outs, (hidden, turned, cots, grads, sem, sem_out) = rest[:4], rest[4:]

    def chunk_at(r):
        return pl.ds(pl.multiple_of(r * CHUNK, CHUNK), CHUNK)

    def chunk_of(r):
        return lat[chunk_at(r), :].astype(jnp.float32)

    def fold(value):
        return jnp.sum(value.reshape(CHUNK // 8, 8, CHANS), axis=0)

    chunks = PIXELS // CHUNK
    zeros = jnp.zeros((8, CHANS), jnp.float32)
    center = group_mean(lax.fori_loop(0, chunks, lambda r, s: s + fold(chunk_of(r)), zeros))

    def squares(r, s):
        off = chunk_of(r) - center
        return s + fold(off * off)

    var = group_mean(lax.fori_loop(0, chunks, squares, zeros))
    slope = lax.rsqrt(var + 1e-05) * affine[0:1, :]
    shift = affine[1:2, :]

    @pl.loop(0, chunks)
    def _(r):
        halved = 0.5 * ((chunk_of(r) - center) * slope + shift)
        rounded = (halved + halved * jnp.tanh(halved)).astype(jnp.bfloat16)
        hidden[chunk_at(r), :] = rounded
        turned[:, chunk_at(r)] = rounded.T

    spread_rows(cot, cots, True)
    keep = [
        pltpu.make_async_copy(hidden, hidden_out, sem_out.at[0]),
        pltpu.make_async_copy(turned, turned_out, sem_out.at[1]),
    ]
    for copy in keep:
        copy.start()
    grad_half(1, turned, cots, grads, outs, sem)
    for copy in keep:
        copy.wait()


def rest_grad_kernel(turned, cot, *rest):
    outs, (cots, grads, sem) = rest[:4], rest[4:]
    spread_rows(cot, cots, True)
    grad_half(0, turned, cots, grads, outs, sem)


def spread_kernel(hidden, taps):
    spread_rows(hidden, taps, False)


GRAD_SCRATCH = [
    pltpu.VMEM((PADDED, SPAN), jnp.bfloat16),
    pltpu.VMEM((5 * CHANS, CHANS), jnp.bfloat16),
    pltpu.SemaphoreType.DMA((4,)),
]
TILE = 8
WINDOW = 7 * 128
CHUNK = 256
SHORT = pl.CostEstimate(flops=10**6, bytes_accessed=10**5, transcendentals=0)
IN_VMEM = pl.BlockSpec(memory_space=pltpu.VMEM)
IN_ANY = pl.BlockSpec(memory_space=pl.ANY)


def norm_grad(latents, cotangent, gain, bias):
    return pl.pallas_call(
        norm_grad_kernel,
        out_shape=[
            jax.ShapeDtypeStruct((PIXELS, CHANS), jnp.bfloat16),
            jax.ShapeDtypeStruct((CHANS, PIXELS), jnp.bfloat16),
        ] + [jax.ShapeDtypeStruct((ROWS, CHANS), jnp.bfloat16)] * 4,
        in_specs=[IN_VMEM] * 3,
        out_specs=[IN_ANY] * 6,
        scratch_shapes=[
            pltpu.VMEM((PIXELS, CHANS), jnp.bfloat16),
            pltpu.VMEM((CHANS, PIXELS), jnp.bfloat16),
        ] + GRAD_SCRATCH + [pltpu.SemaphoreType.DMA((2,))],
        compiler_params=pltpu.CompilerParams(vmem_limit_bytes=58 * MIB),
        cost_estimate=SHORT,
        name="norm_grad",
    )(latents, cotangent, jnp.stack([gain, bias]))


def rest_grad(turned, cotangent):
    return pl.pallas_call(
        rest_grad_kernel,
        out_shape=[jax.ShapeDtypeStruct((ROWS, CHANS), jnp.bfloat16)] * 4,
        in_specs=[IN_VMEM] * 2,
        out_specs=[IN_ANY] * 4,
        scratch_shapes=GRAD_SCRATCH,
        compiler_params=pltpu.CompilerParams(vmem_limit_bytes=58 * MIB),
        cost_estimate=SHORT,
        name="rest_grad",
    )(turned, cotangent)


def spread(hidden):
    return pl.pallas_call(
        spread_kernel,
        out_shape=jax.ShapeDtypeStruct((PADDED, SPAN), jnp.bfloat16),
        in_specs=[IN_VMEM],
        out_specs=IN_VMEM,
        compiler_params=pltpu.CompilerParams(vmem_limit_bytes=20 * MIB),
        cost_estimate=SHORT,
        name="spread",
    )(hidden)


def conv_kernel(places, added, tall, *refs):
    steps = PIXELS // tall
    count = len(places)
    taps_hbm, pieces, refs = refs[0], refs[1 : 1 + count], refs[1 + count :]
    before_hbm = lat_hbm = None
    last = added == 2
    if added:
        before_hbm, refs = refs[0], refs[1:]
    if last:
        lat_hbm, refs = refs[0], refs[1:]
    out_hbm, taps, weights, before, lat, out, sem_w, sem_in, sem_out = refs

    def rows_of(m):
        return pl.ds(pl.multiple_of(m * tall, tall), tall)

    def inputs(m):
        rows = pl.ds(pl.multiple_of(m * tall + 2 * WIDTH, 2 * WIDTH), tall)
        found = [pltpu.make_async_copy(taps_hbm.at[rows], taps.at[rows], sem_in.at[3 * m])]
        rows = rows_of(m)
        if added:
            found.append(pltpu.make_async_copy(before_hbm.at[rows], before.at[rows], sem_in.at[3 * m + 1]))
        if last:
            found.append(pltpu.make_async_copy(lat_hbm.at[rows], lat.at[rows], sem_in.at[3 * m + 2]))
        return found

    def result(m):
        return pltpu.make_async_copy(out.at[rows_of(m)], out_hbm.at[rows_of(m)], sem_out.at[m])

    weights[...] = jnp.zeros_like(weights)
    head = pl.ds(0, 2 * WIDTH)
    copies = [pltpu.make_async_copy(taps_hbm.at[head], taps.at[head], sem_in.at[3 * steps])]
    copies[0].start()
    tiles = []
    blocks = list(dict.fromkeys(place[:2] for place in places))
    for j, (dy, dz, row, rows) in enumerate(places):
        block = block_at(dy, dz)
        base = block * ROWS // 128
        slot = blocks.index((dy, dz)) * WINDOW
        to = pl.ds(pl.multiple_of(slot + block * ROWS - base * 128 + row, 16), rows)
        copies.append(pltpu.make_async_copy(pieces[j], weights.at[to], sem_w.at[j]))
        copies[-1].start()
        if row == 0:
            for k in range(WINDOW // 128):
                tile = jnp.minimum(base + k, KROWS // 128 - 1)
                a = tile // (SPAN // 128)
                tiles.append((a * WIDTH, pl.multiple_of(tile * 128 - a * SPAN, 128)))
    for copy in inputs(0):
        copy.start()
    for copy in copies + inputs(0):
        copy.wait()
    for m in range(1, steps):
        for copy in inputs(m):
            copy.start()

    @pl.loop(0, steps)
    def _(m):
        @pl.when(m > 0)
        def _():
            for copy in inputs(m):
                copy.wait()

        left = jnp.concatenate([
            taps[pl.ds(pl.multiple_of(m * tall + down, WIDTH), tall), pl.ds(lane, 128)]
            for down, lane in tiles
        ], axis=1)
        total = jnp.dot(left, weights[...], preferred_element_type=jnp.float32)
        if added:
            total += before[rows_of(m), :].astype(jnp.float32)
        if last:
            total = lat[rows_of(m), :].astype(jnp.float32) + SCALE * total
        out[rows_of(m), :] = total.astype(jnp.bfloat16)
        result(m).start()

    for m in range(steps):
        result(m).wait()


def conv(taps, places, pieces, others=(), tall=None):
    blocks = len(set(place[:2] for place in places))
    tall = tall or (256 if blocks > 2 else 512)
    return pl.pallas_call(
        partial(conv_kernel, places, len(others), tall),
        out_shape=jax.ShapeDtypeStruct((PIXELS, CHANS), jnp.bfloat16),
        in_specs=[IN_ANY] * (1 + len(pieces) + len(others)),
        out_specs=IN_ANY,
        scratch_shapes=[
            pltpu.VMEM((PADDED, SPAN), jnp.bfloat16),
            pltpu.VMEM((blocks * WINDOW, CHANS), jnp.bfloat16),
            pltpu.VMEM((PIXELS, CHANS), jnp.bfloat16),
            pltpu.VMEM((PIXELS, CHANS), jnp.bfloat16),
            pltpu.VMEM((PIXELS, CHANS), jnp.bfloat16),
            pltpu.SemaphoreType.DMA((len(pieces),)),
            pltpu.SemaphoreType.DMA((3 * (PIXELS // tall) + 1,)),
            pltpu.SemaphoreType.DMA((PIXELS // tall,)),
        ],
        compiler_params=pltpu.CompilerParams(vmem_limit_bytes=58 * MIB),
        cost_estimate=SHORT,
        name="conv",
    )(taps, *pieces, *others)


def together(values, *others):
    return lax.optimization_barrier(tuple(values) + others)[: len(values)]


def from_switch(step, branch, *state):
    return lax.switch(step[0] % 4, [partial(branch, 1 << level) for level in range(4)], *state)


def partner_and_conv(by, chosen, own, other, taps, w_m, w_p):
    w_partner = weight_from_partner(chosen, by)
    places = [(0, 0, 0, ROWS), (1, 0, 0, ROWS), (0, 3, 0, ROWS), (0, 1, 0, ROWS)]
    return w_partner, conv(taps, places, (own, other, w_m, w_p))


def join_kernel(top, bottom, both):
    both[0:HALF, :] = top[...]
    both[HALF:ROWS, :] = bottom[...]


def added(rows, *refs):
    return sum(ref[rows, :].astype(jnp.float32) for ref in refs).astype(jnp.bfloat16)


def sums_kernel(a_y, g02, a_p, a_m, g10, w_m, w_p, far_top, far_bottom, near, w_top, w_bottom):
    far_top[...] = added(slice(0, HALF), a_y, g02)
    far_bottom[...] = added(slice(HALF, ROWS), a_y, g02)
    near[...] = added(slice(0, ROWS), a_p, a_m, g10)
    w_top[...] = w_m[0:HALF, :]
    w_bottom[...] = w_p[HALF:ROWS, :]


def ends_kernel(b_up, g0p, b_dn, g0m, to_up, to_dn):
    to_up[0:HALF, :] = added(slice(0, HALF), b_up, g0p)
    to_up[HALF:ROWS, :] = g0p[HALF:ROWS, :]
    to_dn[0:HALF, :] = g0m[0:HALF, :]
    lower = b_dn[...].astype(jnp.float32) + g0m[HALF:ROWS, :].astype(jnp.float32)
    to_dn[HALF:ROWS, :] = lower.astype(jnp.bfloat16)


def small(kernel, name, rows, *values):
    return pl.pallas_call(
        kernel,
        out_shape=[jax.ShapeDtypeStruct((count, CHANS), jnp.bfloat16) for count in rows],
        in_specs=[IN_VMEM] * len(values),
        out_specs=[IN_VMEM] * len(rows),
        compiler_params=pltpu.CompilerParams(vmem_limit_bytes=20 * MIB),
        cost_estimate=SHORT,
        name=name,
    )(*values)


def moved_kernel(moment, g00, b_y, c_up, c_dn, moved, rounded):
    grad = sum(ref[...].astype(jnp.float32) for ref in (g00, b_y, c_up, c_dn))
    value = 0.9 * moment[...] + grad
    moved[...] = value
    rounded[...] = value.astype(jnp.bfloat16)


def moved_rows(*values):
    rows = pl.BlockSpec((ROWS // 3, CHANS), lambda i: (i, 0))
    return pl.pallas_call(
        moved_kernel,
        out_shape=[jax.ShapeDtypeStruct((ROWS, CHANS), kind) for kind in (jnp.float32, jnp.bfloat16)],
        grid=(3,),
        in_specs=[rows] * 5,
        out_specs=[rows] * 2,
        compiler_params=pltpu.CompilerParams(vmem_limit_bytes=20 * MIB),
        cost_estimate=SHORT,
        name="moved",
    )(*values)


def finish(by, rounded, moved, own_weight, w_partner, taps, w_far, corner, acc):
    partner = from_partner(rounded, by).astype(jnp.float32)
    both = moved + partner
    new_moment = 0.5 * both
    new_weight = 0.5 * (own_weight + w_partner.astype(jnp.float32)) - 0.025 * both
    return new_weight, new_moment, conv(
        taps, [(0, 2, 0, ROWS), (1, 2, 0, ROWS)], (w_far, corner), (acc,), 256
    )


def on_device(latents, cotangent, gain, bias, weight, momentum, step):
    latents, cotangent, own_weight, own_moment = latents[0], cotangent[0], weight[0], momentum[0]
    own = own_weight.astype(jnp.bfloat16)
    w_y = send_inner(own, 1, 0)
    w_m = send_inner(own, 0, 1)
    w_p = send_inner(own, 0, -1)
    latents, cotangent = together((latents, cotangent), own)
    hidden, turned, g10, g1p, g1m, g12 = norm_grad(latents, cotangent, gain, bias)
    g12, g1p, g1m, w_m, w_p, w_y = together((g12, g1p, g1m, w_m, w_p, w_y))
    a_y = send_inner(g12, 1, 0)
    a_p = send_inner(g1p, 0, 1)
    a_m = send_inner(g1m, 0, -1)
    g00, g0p, g0m, g02 = rest_grad(turned, cotangent)
    hidden = together((hidden,), g02)[0]
    taps = spread(hidden)
    a_y, a_p, a_m, taps = together((a_y, a_p, a_m, taps))
    far_top, far_bottom, near, w_top, w_bottom = small(
        sums_kernel, "sums", (HALF, ROWS - HALF, ROWS, HALF, ROWS - HALF),
        a_y, g02, a_p, a_m, g10, w_m, w_p,
    )
    b_up = send_inner(far_top, 0, 1)
    b_dn = send_inner(far_bottom, 0, -1)
    b_y = send_inner(near, 1, 0)
    top = send_inner(w_top, 0, 1)
    bottom = send_inner(w_bottom, 0, -1)
    own_late, w_y_late = together((own, w_y), far_top)
    chosen = to_send(own_late, w_y_late, step)
    b_up, b_dn, chosen = together((b_up, b_dn, chosen))
    to_up, to_dn = small(ends_kernel, "ends", (ROWS, ROWS), b_up, g0p, b_dn, g0m)
    c_up = send_inner(to_up, 0, 1)
    c_dn = send_inner(to_dn, 0, -1)
    taps, top, bottom, b_y = together((taps, top, bottom, b_y), to_up, to_dn)
    w_far, = small(join_kernel, "join", (ROWS,), top, bottom)
    corner = send_inner(w_far, 1, 0)
    w_partner, acc = from_switch(
        step, partner_and_conv, chosen, own, w_y, taps, w_m, w_p
    )
    w_y = together((w_y,), acc)[0]
    y_m = send_inner(w_y, 0, 1)
    y_p = send_inner(w_y, 0, -1)
    moved, rounded = moved_rows(own_moment, g00, b_y, c_up, c_dn)
    new_weight, new_moment, acc = from_switch(
        step, finish, rounded, moved, own_weight, w_partner, taps, w_far, corner, acc
    )
    y_m, y_p = together((y_m, y_p), new_weight, new_moment)
    block_out = conv(taps, [(1, 3, 0, ROWS), (1, 1, 0, ROWS)], (y_m, y_p), (acc, latents))
    return (block_out[None], new_weight[None], new_moment[None])


def solution(mesh):
    placed = (
        P(("group", "inner"), None, None),
        P(("group", "inner"), None, None),
        P(),
        P(),
        P("group", "inner", None),
        P("group", "inner", None),
        P(),
    )
    return jax.shard_map(
        on_device,
        mesh=mesh,
        in_specs=placed,
        out_specs=(
            P(("group", "inner"), None, None),
            P("group", "inner", None),
            P("group", "inner", None),
        ),
        check_vma=False,
    )
```
